256 devices in a mesh: row: 16 (over z_lo, x, core), col: 16 (over z_hi, y).
Axes of the slice: x: 4, y: 4, z: 8 (z_hi: 4, z_lo: 2; z = z_hi * 2 + z_lo), core: 2. Of those that a mesh axis runs over, the one named last changes fastest.
Arguments:
- activations: bfloat16 [1152, 28672], P('row', 'col'), may hold values from -6 to 6
- grad_outputs: bfloat16 [1152, 8192], P('col', 'row'), may hold values from -6 to 6
- input_basis: bfloat16 [28672, 28672], P('col', 'row'), may hold values from -0.03125 to 0.03125
- output_basis: bfloat16 [8192, 8192], P('row', 'col'), may hold values from -0.0625 to 0.0625
- segment_ids: int32 [1152], replicated, may hold values from 0 to 2, never falling along the last dimension, each value on 1 to 576 neighbouring positions
Outputs:
- correction: float32 [28672, 8192], P('row', 'col')
The draws below stay inside these ranges and needn't reach their ends.
Inputs may be any that keep to these rules, and one draw needn't show every extreme that they name: `segment_ids`: segment ids never fall along the tokens; each of the 3 sequences has 1 to 576 tokens, one exactly 576.
All inputs are finite; a program needn't handle non-finite values.
Results may differ from the reference program's by a relative error of at most 0.0037.
Values may be sent and summed in bfloat16 or wider, within the bound.
A program may use at most 64 MiB of HBM per device.

```python
import math
import jax
import jax.numpy as jnp
import numpy as np
from jax import lax

DIN = 28672
DOUT = 8192
TOKENS = 1152
NSEQ = 3
SEQ_MOST = 576


def block_scale(rng, dims, cuts, smallest, largest):
    def one(axis_at, shards_of):
        draws = jax.random.uniform(jax.random.fold_in(jax.random.fold_in(rng, 6), axis_at), (shards_of,), jnp.float32, smallest / len(cuts), largest / len(cuts))
        return jnp.repeat(jnp.exp(draws), dims[axis_at] // shards_of).reshape((-1,) + (1,) * (len(dims) - axis_at - 1))

    loudness = one(*cuts[0])
    for cut in cuts[1:]:
        loudness = loudness * one(*cut)
    return loudness


def length_profile(amount, total, limit, skew):
    weights = [(1 << 20) // math.isqrt(grade ** skew) + 1 for grade in range(2, amount + 1)]
    rest, holding = total - limit - (amount - 1), [1] * (amount - 1)
    while rest > 0:
        candidates = [i for i in range(amount - 1) if holding[i] < limit]
        mass, budget = sum([weights[i] for i in candidates]), rest
        for i in candidates:
            more = min(limit - holding[i], max(1, budget * weights[i] // mass), rest)
            holding[i] = holding[i] + more
            rest = rest - more
    return np.array([limit] + holding)


def uneven_parts(rng, number_of, total, bound, slope):
    if number_of == 2:
        one = jax.random.randint(rng, (), max(1, total - bound), min(bound, total - 1) + 1)
        return jnp.stack([one, total - one])
    tallies = jnp.asarray(length_profile(number_of, total, bound, slope), jnp.int32)
    pairs = (number_of - 1) // 2
    source_of, sink = tallies[1:1 + 2 * pairs:2], tallies[2:2 + 2 * pairs:2]
    slack = jnp.minimum(source_of - 1, bound - sink)
    passed = jax.random.randint(jax.random.fold_in(rng, 1), (pairs,), 0, 1 << 20) % (slack + 1)
    tallies = tallies.at[1:1 + 2 * pairs:2].set(source_of - passed).at[2:2 + 2 * pairs:2].set(sink + passed)
    return tallies[jax.random.permutation(jax.random.fold_in(rng, 2), number_of)]


def gaussian(key, extent, scale, most, cuts=(), held_as=jnp.bfloat16):
    values = scale * jax.random.normal(key, extent, jnp.float32)
    if cuts:
        values = values * block_scale(key, extent, cuts, -0.22, 0.18)
    return jnp.clip(values, -most, most).astype(held_as)


def setup_inputs(seed: int = 0) -> dict:
    key_list = jax.random.split(jax.random.key(seed), 6)
    return {
        "activations": gaussian(key_list[0], (TOKENS, DIN), 1.0, 6.0, ((0, 16), (1, 16))),
        "grad_outputs": gaussian(key_list[1], (TOKENS, DOUT), 1.0, 6.0, ((0, 16), (1, 16))),
        "input_basis": gaussian(key_list[2], (DIN, DIN), DIN ** -0.5, 0.03125, ((0, 16), (1, 16))),
        "output_basis": gaussian(key_list[3], (DOUT, DOUT), DOUT ** -0.5, 0.0625, ((0, 16), (1, 16))),
        "segment_ids": jnp.searchsorted(jnp.cumsum(uneven_parts(key_list[4], NSEQ, TOKENS, SEQ_MOST, 1)), jnp.arange(TOKENS), side="right").astype(jnp.int32),
    }


def reference(activations, grad_outputs, input_basis, output_basis, segment_ids):
    act_rot = jnp.dot(activations, input_basis, preferred_element_type=jnp.float32).astype(jnp.bfloat16)
    grad_rot = jnp.dot(grad_outputs, output_basis, preferred_element_type=jnp.float32).astype(jnp.bfloat16)
    labels = jnp.arange(NSEQ, dtype=jnp.int32)
    onehot = (segment_ids[None, :] == labels[:, None])
    counts = jnp.sum(onehot.astype(jnp.float32), axis=1)
    act_cols = act_rot.T

    def accumulate(running, index):
        member = onehot[index].astype(jnp.bfloat16)
        masked = grad_rot * member[:, None]
        per_seq = jnp.dot(act_cols, masked, preferred_element_type=jnp.float32)
        scale = 1.0 / (counts[index] * NSEQ)
        return running + per_seq * per_seq * scale, None

    start_value = jnp.zeros((DIN, DOUT), jnp.float32)
    result, _ = lax.scan(accumulate, start_value, labels)
    return result
```

```python
import jax
import jax.numpy as jnp
from jax import lax
from jax.experimental import pallas as pl
from jax.experimental.pallas import tpu as pltpu
from jax.sharding import PartitionSpec as P

MESH = pl.DeviceIdType.MESH
NSEQ = 3
TOK = 1152
SLAB = 72
CIN = 1792
GIN = 512
STEPS = 7
WIDE = 256
QUARTER = 64
HALF = 32
PIECE = 16
TILE = 384
BF = jnp.bfloat16
F32 = jnp.float32


def kernel(
    act, grad, basis, obasis, ids, out,
    slabs, acts, bas, obas, part, half_out, half_in, full_out, full_in, z_out, z_in, rot, res,
    gslabs, gpart, gcore, gin, grot,
    send, recv, asend, arecv, gsend, grecv, local,
):
    r, c = lax.axis_index("row"), lax.axis_index("col")
    core, x, zl = r % 2, (r // 2) % 4, r // 8
    y, zh = c % 4, c // 4
    chip = zl * 4 + x

    def row_dev(x_, zl_, core_):
        return {"row": zl_ * 8 + x_ * 2 + core_, "col": c}

    def col_dev(y_, zh_):
        return {"row": r, "col": zh_ * 4 + y_}

    twin = row_dev(x, zl, 1 - core)
    x_up, x_dn = row_dev((x + 1) % 4, zl, core), row_dev((x + 3) % 4, zl, core)
    z_pair = row_dev(x, 1 - zl, core)
    y_up, y_dn = col_dev((y + 1) % 4, zh), col_dev((y + 3) % 4, zh)

    def chip_dev(k):
        return {"row": k * 2 + core, "col": c}

    barrier = pltpu.get_barrier_semaphore()
    for dev in [twin, y_up, y_dn] + [col_dev(y, (zh + o) % 4) for o in (1, 2, 3)] + [
        chip_dev((chip + o) % 8) for o in range(1, 8)
    ]:
        pl.semaphore_signal(barrier, inc=1, device_id=dev, device_id_type=MESH)
    pl.semaphore_wait(barrier, 13)

    def remote(src, dst, s, d, dev):
        return pltpu.make_async_remote_copy(
            src_ref=src, dst_ref=dst, send_sem=s, recv_sem=d, device_id=dev, device_id_type=MESH
        )

    own_act = pltpu.make_async_copy(act, slabs.at[r], local.at[0])
    own_grad = pltpu.make_async_copy(grad, gslabs.at[c], local.at[1])
    own_act.start()
    own_grad.start()
    own_ob = pltpu.make_async_copy(obasis, obas, local.at[2])
    own_ob.start()

    def basis_copy(j):
        return pltpu.make_async_copy(
            basis.at[:, pl.ds(pl.multiple_of(j * WIDE, WIDE), WIDE)], bas.at[j], local.at[3 + j]
        )

    def slab_at(x_, zl_, core_):
        return slabs.at[zl_ * 8 + x_ * 2 + core_]

    LO, HI = slice(0, CIN // 2), slice(CIN // 2, CIN)

    def ship(n, src, dst, dev):
        d = remote(src, dst, asend.at[n], arecv.at[n], dev)
        d.start()

    def landed(n, dst, dev):
        remote(dst, dst, asend.at[n], arecv.at[n], dev).wait_recv()

    xm, xp, xo, zo = (x + 3) % 4, (x + 1) % 4, (x + 2) % 4, 1 - zl
    mine = slabs.at[r]

    ship(0, act, mine, z_pair)
    ship(1, act, mine, x_up)
    ship(2, act, mine, x_dn)
    ship(9, act, mine, twin)

    def gship(n, src, dst, dev):
        remote(src, dst, gsend.at[n], grecv.at[n], dev).start()

    def glanded(n, dst, dev):
        remote(dst, dst, gsend.at[n], grecv.at[n], dev).wait_recv()

    for o in (1, 2, 3):
        h = (zh + o) % 4
        remote(grad, gslabs.at[c], gsend.at[h], grecv.at[zh], col_dev(y, h)).start()

    for j in range(STEPS):
        basis_copy(j).start()

    landed(0, slab_at(x, zo, core), z_pair)
    ship(3, slab_at(x, zo, core), slab_at(x, zo, core), x_up)
    ship(4, slab_at(x, zo, core), slab_at(x, zo, core), x_dn)
    ship(10, slab_at(x, zo, core), slab_at(x, zo, core), twin)

    own_grad.wait()
    for o in (1, 2, 3):
        h = (zh + o) % 4
        glanded(h, gslabs.at[h * 4 + y], col_dev(y, h))
    for h in range(4):
        piece = gslabs.at[h * 4 + y]
        gship(4 + h, piece, piece, y_up)
        gship(8 + h, piece, piece, y_dn)

    def relay(n_up, n_dn, n_half_up, n_half_dn, n_twin_m, n_twin_p, zl_):
        below, above = slab_at(xm, zl_, core), slab_at(xp, zl_, core)
        landed(n_up, below, x_dn)
        ship(n_half_up, below.at[:, LO], below.at[:, LO], x_up)
        ship(n_twin_m, below, below, twin)
        landed(n_dn, above, x_up)
        ship(n_half_dn, above.at[:, HI], above.at[:, HI], x_dn)
        ship(n_twin_p, above, above, twin)

    relay(1, 2, 5, 6, 11, 12, zl)

    for h in range(4):
        glanded(4 + h, gslabs.at[h * 4 + (y + 3) % 4], y_dn)
        glanded(8 + h, gslabs.at[h * 4 + (y + 1) % 4], y_up)
    for h in range(2):
        piece = gslabs.at[h * 4 + (y + 3) % 4]
        gship(12 + h, piece, piece, y_up)
        piece = gslabs.at[(2 + h) * 4 + (y + 1) % 4]
        gship(14 + h, piece, piece, y_dn)

    relay(3, 4, 7, 8, 13, 14, zo)

    for n, zl_ in ((5, zl), (7, zo)):
        far = slab_at(xo, zl_, core)
        landed(n, far.at[:, LO], x_dn)
        landed(n + 1, far.at[:, HI], x_up)
        ship(15 if n == 5 else 16, far, far, twin)

    for h in range(2):
        glanded(12 + h, gslabs.at[h * 4 + (y + 2) % 4], y_dn)
        glanded(14 + h, gslabs.at[(2 + h) * 4 + (y + 2) % 4], y_up)
    own_ob.wait()

    def rotate_grad(k, carry):
        a = gslabs[2 * k].astype(F32)
        b = gslabs[2 * k + 1].astype(F32)
        both = jnp.concatenate([a, b], axis=0).astype(BF)
        prod = jnp.dot(both, obas[...], preferred_element_type=F32)
        gpart[0, k] = prod[:, :256]
        gpart[1, k] = prod[:, 256:]
        return carry

    lax.fori_loop(0, 8, rotate_grad, 0)
    gship(16, gpart.at[1 - core], gcore, twin)

    own_act.wait()
    for n, x_, zl_ in (
        (9, x, zl), (10, x, zo), (11, xm, zl), (12, xp, zl), (13, xm, zo), (14, xp, zo), (15, xo, zl), (16, xo, zo),
    ):
        landed(n, slab_at(x_, zl_, 1 - core), twin)

    def join(k, carry):
        a = slabs[2 * k].astype(F32)
        b = slabs[2 * k + 1].astype(F32)
        acts[pl.ds(pl.multiple_of(k * 144, 16), 144), :] = jnp.concatenate([a, b], axis=0).astype(BF)
        return carry

    lax.fori_loop(0, 8, join, 0)

    label = ids[...]
    members = [(label == s) for s in range(NSEQ)]
    weights = [1.0 / (jnp.sum(m.astype(F32), axis=1, keepdims=True) * NSEQ) for m in members]
    masks = [m.astype(F32).astype(BF) for m in members]

    def msg(j, n_send, n_recv, src, dst, dev):
        return remote(src, dst, send.at[j, n_send], recv.at[j, n_recv], dev)

    def stage_compute(j):
        basis_copy(j).wait()

        def tile(m, carry):
            at = pl.multiple_of(m * TILE, TILE)
            prod = jnp.dot(acts[pl.ds(at, TILE), :], bas[j], preferred_element_type=F32)
            part[j, :, :, pl.ds(at, TILE)] = prod.T.reshape(4, QUARTER, TILE)
            return carry

        lax.fori_loop(0, TOK // TILE, tile, 0)
        d = (y + 2) % 4
        half_out[j, 0] = part[j, d, :HALF].astype(BF)
        half_out[j, 1] = part[j, d, HALF:].astype(BF)
        msg(j, 0, 0, half_out.at[j, 0], half_in.at[j, 0], y_up).start()
        msg(j, 1, 1, half_out.at[j, 1], half_in.at[j, 1], y_dn).start()

    def stage_half(j):
        up, dn = (y + 1) % 4, (y + 3) % 4
        msg(j, 0, 0, half_out.at[j, 0], half_in.at[j, 0], y_dn).wait_recv()
        full_out[j, 0, :HALF] = (part[j, up, :HALF] + half_in[j, 0].astype(F32)).astype(BF)
        full_out[j, 0, HALF:] = part[j, up, HALF:].astype(BF)
        msg(j, 2, 2, full_out.at[j, 0], full_in.at[j, 0], y_up).start()
        msg(j, 1, 1, half_out.at[j, 1], half_in.at[j, 1], y_up).wait_recv()
        full_out[j, 1, HALF:] = (part[j, dn, HALF:] + half_in[j, 1].astype(F32)).astype(BF)
        full_out[j, 1, :HALF] = part[j, dn, :HALF].astype(BF)
        msg(j, 3, 3, full_out.at[j, 1], full_in.at[j, 1], y_dn).start()

    def stage_full(j):
        msg(j, 2, 2, full_out.at[j, 0], full_in.at[j, 0], y_dn).wait_recv()
        msg(j, 3, 3, full_out.at[j, 1], full_in.at[j, 1], y_up).wait_recv()
        total = part[j, y] + full_in[j, 0].astype(F32) + full_in[j, 1].astype(F32)
        part[j, y] = total
        z_out[j] = total.astype(BF).reshape(4, PIECE, TOK)
        for o in (1, 2, 3):
            h = (zh + o) % 4
            msg(j, 4 + h, 4 + zh, z_out.at[j, h], z_in.at[j, zh], col_dev(y, h)).start()

    def stage_z(j):
        total = part[j, y, pl.ds(pl.multiple_of(zh * PIECE, PIECE), PIECE), :]
        for o in (1, 2, 3):
            h = (zh + o) % 4
            msg(j, 4 + h, 4 + h, z_out.at[j, h], z_in.at[j, h], col_dev(y, h)).wait_recv()
            total = total + z_in[j, h].astype(F32)
        rot[j, y, zh] = total.astype(BF)
        for o in (1, 2, 3):
            h = (zh + o) % 4
            piece = rot.at[j, y, zh]
            msg(j, 8 + h, 8 + zh, piece, piece, col_dev(y, h)).start()

    def stage_gather(j):
        for o in (1, 2, 3):
            h = (zh + o) % 4
            piece = rot.at[j, y, h]
            msg(j, 8 + h, 8 + h, piece, piece, col_dev(y, h)).wait_recv()
        quarter = rot.at[j, y]
        msg(j, 12, 12, quarter, quarter, y_up).start()
        msg(j, 13, 13, quarter, quarter, y_dn).start()

    def stage_relay(j):
        below, above = rot.at[j, (y + 3) % 4], rot.at[j, (y + 1) % 4]
        msg(j, 12, 12, below, below, y_dn).wait_recv()
        piece = below.at[0:2]
        msg(j, 14, 14, piece, piece, y_up).start()
        msg(j, 13, 13, above, above, y_up).wait_recv()
        piece = above.at[2:4]
        msg(j, 15, 15, piece, piece, y_dn).start()

    def out_copy(j):
        return pltpu.make_async_copy(
            res.at[j], out.at[pl.ds(pl.multiple_of(j * WIDE, WIDE), WIDE), :], local.at[10 + j]
        )

    def stage_out(j):
        far = rot.at[j, (y + 2) % 4]
        msg(j, 14, 14, far.at[0:2], far.at[0:2], y_dn).wait_recv()
        msg(j, 15, 15, far.at[2:4], far.at[2:4], y_up).wait_recv()
        a = rot[j].reshape(WIDE, TOK)
        for h in range(2):
            g = grot[h].reshape(TOK, 256)
            total = None
            for s in range(NSEQ):
                p = jnp.dot(a * masks[s], g, preferred_element_type=F32)
                term = p * p * weights[s]
                total = term if total is None else total + term
            res[j, :, pl.ds(h * 256, 256)] = total
        out_copy(j).start()

    def grad_core():
        glanded(16, gcore, twin)

        def add(k, carry):
            gpart[core, k] = gpart[core, k] + gcore[k]
            return carry

        lax.fori_loop(0, 8, add, 0)
        for o in range(1, 8):
            k = (chip + o) % 8
            remote(gpart.at[core, k], gin.at[chip], gsend.at[17 + k], grecv.at[17 + chip], chip_dev(k)).start()

    def grad_sum():
        total = gpart[core, chip]
        for o in range(1, 8):
            k = (chip + o) % 8
            glanded(17 + k, gin.at[k], chip_dev(k))
            total = total + gin[k]
        grot[core, chip] = total.astype(BF)
        piece = grot.at[core, chip]
        for o in range(1, 8):
            k = (chip + o) % 8
            remote(piece, piece, gsend.at[25 + k], grecv.at[25 + chip], chip_dev(k)).start()

    def grad_gather():
        for o in range(1, 8):
            k = (chip + o) % 8
            glanded(25 + k, grot.at[core, k], chip_dev(k))
        gship(33, grot.at[core], grot.at[core], twin)

    def grad_done():
        glanded(33, grot.at[1 - core], twin)

    stages = [stage_compute, stage_half, stage_full, stage_z, stage_gather, stage_relay, stage_out]
    extras = {1: grad_core, 3: grad_sum, 5: grad_gather, 6: grad_done}

    def turn(t, carry):
        for lag, stage in enumerate(stages):
            if lag == len(stages) - 1:
                for at, extra in extras.items():
                    pl.when(t == at)(extra)

            @pl.when((t >= lag) & (t < lag + STEPS))
            def _():
                stage(t - lag)

        return carry

    lax.fori_loop(0, STEPS + len(stages) - 1, turn, 0)

    def finish(j, carry):
        out_copy(j).wait()
        for n in (0, 1):
            msg(j, n, n, half_out.at[j, n], half_in.at[j, n], y_up).wait_send()
            msg(j, 2 + n, 2 + n, full_out.at[j, n], full_in.at[j, n], y_up).wait_send()
            msg(j, 12 + n, 12 + n, rot.at[j, y], rot.at[j, y], y_up).wait_send()
            msg(j, 14 + n, 14 + n, rot.at[j, y, 0:2], rot.at[j, y, 0:2], y_up).wait_send()
        for o in (1, 2, 3):
            h = (zh + o) % 4
            for base in (4, 8):
                msg(j, base + h, base + h, rot.at[j, y, h], rot.at[j, y, h], col_dev(y, h)).wait_send()
        return carry

    lax.fori_loop(0, STEPS, finish, 0)

    def sent(sem, ref, dev):
        remote(ref, ref, sem, sem, dev).wait_send()

    for n in (0, 1, 2, 3, 4, 9, 10, 11, 12, 13, 14, 15, 16):
        sent(asend.at[n], mine, twin)
    for n in (5, 6, 7, 8):
        sent(asend.at[n], mine.at[:, LO], twin)
    for o in (1, 2, 3):
        sent(gsend.at[(zh + o) % 4], gslabs.at[c], twin)
    for n in range(4, 16):
        sent(gsend.at[n], gslabs.at[c], twin)
    sent(gsend.at[16], gcore, twin)
    for o in range(1, 8):
        k = (chip + o) % 8
        sent(gsend.at[17 + k], gin.at[k], twin)
        sent(gsend.at[25 + k], grot.at[core, k], twin)
    sent(gsend.at[33], grot.at[core], twin)


def shards(activations, grad_outputs, input_basis, output_basis, segment_ids):
    hbm = pl.BlockSpec(memory_space=pl.ANY)
    dma = pltpu.SemaphoreType.DMA
    return pl.pallas_call(
        kernel,
        out_shape=jax.ShapeDtypeStruct((CIN, GIN), F32),
        in_specs=[hbm, hbm, hbm, hbm, pl.BlockSpec(memory_space=pltpu.VMEM)],
        out_specs=hbm,
        scratch_shapes=[
            pltpu.VMEM((16, SLAB, CIN), BF),
            pltpu.VMEM((TOK, CIN), BF),
            pltpu.VMEM((STEPS, CIN, WIDE), BF),
            pltpu.VMEM((GIN, GIN), BF),
            pltpu.VMEM((STEPS, 4, QUARTER, TOK), F32),
            pltpu.VMEM((STEPS, 2, HALF, TOK), BF),
            pltpu.VMEM((STEPS, 2, HALF, TOK), BF),
            pltpu.VMEM((STEPS, 2, QUARTER, TOK), BF),
            pltpu.VMEM((STEPS, 2, QUARTER, TOK), BF),
            pltpu.VMEM((STEPS, 4, PIECE, TOK), BF),
            pltpu.VMEM((STEPS, 4, PIECE, TOK), BF),
            pltpu.VMEM((STEPS, 4, 4, PIECE, TOK), BF),
            pltpu.VMEM((STEPS, WIDE, GIN), F32),
            pltpu.VMEM((16, SLAB, GIN), BF),
            pltpu.VMEM((2, 8, 144, 256), F32),
            pltpu.VMEM((8, 144, 256), F32),
            pltpu.VMEM((8, 144, 256), F32),
            pltpu.VMEM((2, 8, 144, 256), BF),
            dma((STEPS, 16)),
            dma((STEPS, 16)),
            dma((17,)),
            dma((17,)),
            dma((34,)),
            dma((34,)),
            dma((17,)),
        ],
        compiler_params=pltpu.CompilerParams(
            collective_id=0, has_side_effects=True, vmem_limit_bytes=60 * 1024 * 1024
        ),
        cost_estimate=pl.CostEstimate(flops=15_000_000_000, bytes_accessed=16_000_000, transcendentals=0),
    )(activations, grad_outputs, input_basis, output_basis, segment_ids.reshape(1, TOK))


def solution(mesh):
    placed = (P("row", "col"), P("col", "row"), P("col", "row"), P("row", "col"), P())
    return jax.shard_map(
        shards, mesh=mesh, in_specs=placed, out_specs=P("row", "col"), check_vma=False
    )
```

```python
import jax
import jax.numpy as jnp
from jax import lax
from jax.experimental import pallas as pl
from jax.experimental.pallas import tpu as pltpu
from jax.sharding import PartitionSpec as P

MESH = pl.DeviceIdType.MESH
NSEQ = 3
TOK = 1152
SLAB = 72
CIN = 1792
GIN = 512
STEPS = 7
WIDE = 256
QUARTER = 64
HALF = 32
PIECE = 16
LANES = ((0, 512), (512, 640))
LEAD = 2
GDONE = 26
LAGS = (0, 2, 4, 7, 10, 12, 14)
BF = jnp.bfloat16
F32 = jnp.float32


def kernel(
    act, grad, basis, obasis, ids, out,
    slabs, acts, bas, obas, part, half_out, half_in, full_out, full_in, z_out, z_in, rot, res,
    gslabs, gpart, gcore, gin, gpair, grot, gmask, labels,
    send, recv, asend, arecv, gsend, grecv, local,
):
    r, c = lax.axis_index("row"), lax.axis_index("col")
    core, x, zl = r % 2, (r // 2) % 4, r // 8
    y, zh = c % 4, c // 4

    def row_dev(x_, zl_, core_):
        return {"row": zl_ * 8 + x_ * 2 + core_, "col": c}

    def col_dev(y_, zh_):
        return {"row": r, "col": zh_ * 4 + y_}

    twin = row_dev(x, zl, 1 - core)
    x_up, x_dn = row_dev((x + 1) % 4, zl, core), row_dev((x + 3) % 4, zl, core)
    z_pair = row_dev(x, 1 - zl, core)
    y_up, y_dn = col_dev((y + 1) % 4, zh), col_dev((y + 3) % 4, zh)

    x_far = row_dev((x + 2) % 4, zl, core)

    barrier = pltpu.get_barrier_semaphore()
    for dev in [twin, x_up, x_dn, z_pair, x_far, y_up, y_dn] + [col_dev(y, (zh + o) % 4) for o in (1, 2, 3)]:
        pl.semaphore_signal(barrier, inc=1, device_id=dev, device_id_type=MESH)
    pl.semaphore_wait(barrier, 10)

    def remote(src, dst, s, d, dev):
        return pltpu.make_async_remote_copy(
            src_ref=src, dst_ref=dst, send_sem=s, recv_sem=d, device_id=dev, device_id_type=MESH
        )

    own_act = pltpu.make_async_copy(act, slabs.at[r], local.at[0])
    own_grad = pltpu.make_async_copy(grad, gslabs.at[zh, y], local.at[1])
    own_act.start()
    own_grad.start()
    own_ob = pltpu.make_async_copy(obasis, obas, local.at[2])
    own_ob.start()

    def basis_copy(j):
        return pltpu.make_async_copy(
            basis.at[:, pl.ds(pl.multiple_of(j * WIDE, WIDE), WIDE)], bas.at[j], local.at[3 + j]
        )

    def slab_at(x_, zl_, core_):
        return slabs.at[zl_ * 8 + x_ * 2 + core_]

    LO, HI = slice(0, CIN // 2), slice(CIN // 2, CIN)

    def ship(n, src, dst, dev):
        d = remote(src, dst, asend.at[0], arecv.at[n], dev)
        d.start()

    def landed(n, dst, dev):
        remote(dst, dst, asend.at[0], arecv.at[n], dev).wait_recv()

    xm, xp, xo, zo = (x + 3) % 4, (x + 1) % 4, (x + 2) % 4, 1 - zl
    mine = slabs.at[r]

    ship(0, act, mine, z_pair)
    ship(1, act, mine, x_up)
    ship(2, act, mine, x_dn)
    ship(9, act, mine, twin)

    def gship(n, src, dst, dev):
        remote(src, dst, gsend.at[n], grecv.at[n], dev).start()

    def glanded(n, dst, dev):
        remote(dst, dst, gsend.at[n], grecv.at[n], dev).wait_recv()

    for j in range(STEPS):
        basis_copy(j).start()

    landed(0, slab_at(x, zo, core), z_pair)
    ship(3, slab_at(x, zo, core), slab_at(x, zo, core), x_up)
    ship(4, slab_at(x, zo, core), slab_at(x, zo, core), x_dn)
    ship(10, slab_at(x, zo, core), slab_at(x, zo, core), twin)

    for o in (1, 2, 3):
        h = (zh + o) % 4
        remote(grad, gslabs.at[zh, y], gsend.at[0], grecv.at[0], col_dev(y, h)).start()

    below, above, far = slab_at(xm, zl, core), slab_at(xp, zl, core), slab_at(xo, zl, core)
    landed(1, below, x_dn)
    ship(5, below.at[:, LO], below.at[:, LO], x_up)
    ship(11, below, below, twin)
    landed(2, above, x_up)
    ship(6, above.at[:, HI], above.at[:, HI], x_dn)
    ship(12, above, above, twin)

    order = ((x, zl), (x, zo), (xm, zl), (xp, zl), (xo, zl), (xm, zo), (xp, zo), (xo, zo))

    def join(i):
        k = order[i][1] * 4 + order[i][0]
        a = slabs[2 * k].astype(F32)
        b = slabs[2 * k + 1].astype(F32)
        acts[pl.ds(i * 144, 144), :] = jnp.concatenate([a, b], axis=0).astype(BF)

    own_act.wait()
    for n, i in ((9, 0), (10, 1), (11, 2), (12, 3)):
        landed(n, slab_at(*order[i], 1 - core), twin)
        join(i)

    def act_far():
        landed(5, far.at[:, LO], x_dn)
        landed(6, far.at[:, HI], x_up)
        ship(7, far, far, z_pair)
        ship(15, far, far, twin)

    def act_cross():
        for n, x_, dev, out_n in ((3, xm, x_dn, 13), (4, xp, x_up, 14)):
            landed(n, slab_at(x_, zo, core), dev)
            ship(out_n, slab_at(x_, zo, core), slab_at(x_, zo, core), twin)

    def act_last():
        landed(7, slab_at(xo, zo, core), z_pair)
        ship(16, slab_at(xo, zo, core), slab_at(xo, zo, core), twin)
        for n, i in ((15, 4), (13, 5), (14, 6), (16, 7)):
            landed(n, slab_at(*order[i], 1 - core), twin)
            join(i)

    label = ids[...].reshape(1, TOK)
    weights = [
        1.0 / (jnp.sum((label == s).astype(F32), axis=1, keepdims=True) * NSEQ) for s in range(NSEQ)
    ]
    labels[...] = jnp.broadcast_to(label.astype(F32), (128, TOK)).T

    up, dn, op = (y + 1) % 4, (y + 3) % 4, (y + 2) % 4
    others = [(zh + o) % 4 for o in (1, 2, 3)]

    def msg(j, m, n_send, n_recv, src, dst, dev):
        return remote(src, dst, send.at[n_send], recv.at[j, m, n_recv], dev)

    def lanes(m):
        return pl.ds(*LANES[m])

    def stage_compute(j, m):
        ln = lanes(m)
        if m == 0:
            basis_copy(j).wait()
        prod = jnp.dot(acts[ln, :], bas[j], preferred_element_type=F32)
        part[j, :, :, ln] = prod.T.reshape(4, QUARTER, LANES[m][1])
        half_out[j, 0, :, ln] = part[j, op, :HALF, ln].astype(BF)
        half_out[j, 1, :, ln] = part[j, op, HALF:, ln].astype(BF)
        for n, dev in ((0, y_up), (1, y_dn)):
            msg(j, m, 0, n, half_out.at[j, n, :, ln], half_in.at[j, n, :, ln], dev).start()

    def stage_half(j, m):
        ln = lanes(m)
        msg(j, m, 0, 0, half_out.at[j, 0, :, ln], half_in.at[j, 0, :, ln], y_dn).wait_recv()
        full_out[j, 0, :HALF, ln] = (part[j, up, :HALF, ln] + half_in[j, 0, :, ln].astype(F32)).astype(BF)
        full_out[j, 0, HALF:, ln] = part[j, up, HALF:, ln].astype(BF)
        msg(j, m, 1, 2, full_out.at[j, 0, :, ln], full_in.at[j, 0, :, ln], y_up).start()
        msg(j, m, 0, 1, half_out.at[j, 1, :, ln], half_in.at[j, 1, :, ln], y_up).wait_recv()
        full_out[j, 1, HALF:, ln] = (part[j, dn, HALF:, ln] + half_in[j, 1, :, ln].astype(F32)).astype(BF)
        full_out[j, 1, :HALF, ln] = part[j, dn, :HALF, ln].astype(BF)
        msg(j, m, 1, 2, full_out.at[j, 1, :, ln], full_in.at[j, 1, :, ln], y_dn).start()

    def stage_full(j, m):
        ln = lanes(m)
        msg(j, m, 1, 2, full_out.at[j, :, :, ln], full_in.at[j, :, :, ln], y_dn).wait_recv()
        total = part[j, y, :, ln] + full_in[j, 0, :, ln].astype(F32) + full_in[j, 1, :, ln].astype(F32)
        part[j, y, :, ln] = total
        z_out[j, :, :, ln] = total.astype(BF).reshape(4, PIECE, LANES[m][1])
        for h in others:
            msg(j, m, 2, 3, z_out.at[j, h, :, ln], z_in.at[j, zh, :, ln], col_dev(y, h)).start()

    def stage_z(j, m):
        ln = lanes(m)
        total = part[j, y, pl.ds(pl.multiple_of(zh * PIECE, PIECE), PIECE), ln]
        msg(j, m, 2, 3, z_out.at[j, 0:3, :, ln], z_in.at[j, 0:3, :, ln], y_up).wait_recv()
        for h in others:
            total = total + z_in[j, h, :, ln].astype(F32)
        rot[j, y, zh, :, ln] = total.astype(BF)
        piece = rot.at[j, y, zh, :, ln]
        for h in others:
            msg(j, m, 3, 4, piece, piece, col_dev(y, h)).start()

    def stage_gather(j, m):
        ln = lanes(m)
        pieces = rot.at[j, y, 0:3, :, ln]
        msg(j, m, 3, 4, pieces, pieces, y_up).wait_recv()
        quarter = rot.at[j, y, :, :, ln]
        msg(j, m, 4, 5, quarter, quarter, y_up).start()
        msg(j, m, 4, 6, quarter, quarter, y_dn).start()

    def stage_relay(j, m):
        ln = lanes(m)
        below, above = rot.at[j, dn, :, :, ln], rot.at[j, up, :, :, ln]
        msg(j, m, 4, 5, below, below, y_dn).wait_recv()
        piece = rot.at[j, dn, 0:2, :, ln]
        msg(j, m, 5, 7, piece, piece, y_up).start()
        msg(j, m, 4, 6, above, above, y_up).wait_recv()
        piece = rot.at[j, up, 2:4, :, ln]
        msg(j, m, 5, 7, piece, piece, y_dn).start()

    def stage_last(j, m):
        ln = lanes(m)
        quarter = rot.at[j, op, :, :, ln]
        msg(j, m, 5, 7, quarter, quarter, y_dn).wait_recv()

    def out_copy(j):
        return pltpu.make_async_copy(
            res.at[j], out.at[pl.ds(pl.multiple_of(j * WIDE, WIDE), WIDE), :], local.at[10 + j]
        )

    def square(j):
        a = rot[j].reshape(WIDE, TOK)
        for h in range(2):
            total = None
            for s in range(NSEQ):
                p = jnp.dot(a, gmask[s, h], preferred_element_type=F32)
                term = p * p * weights[s]
                total = term if total is None else total + term
            res[j, :, pl.ds(h * 256, 256)] = total
        out_copy(j).start()

    def grad_y():
        own_grad.wait()
        remote(gslabs.at[0:3, 0], gslabs.at[0:3, 0], gsend.at[0], grecv.at[0], y_up).wait_recv()
        mine_y = gslabs.at[:, y]
        remote(mine_y, mine_y, gsend.at[0], grecv.at[1], y_up).start()
        remote(mine_y, mine_y, gsend.at[0], grecv.at[2], y_dn).start()

    def grad_relay():
        below_y, above_y = gslabs.at[:, dn], gslabs.at[:, up]
        remote(below_y, below_y, gsend.at[0], grecv.at[1], y_dn).wait_recv()
        piece = gslabs.at[0:2, dn]
        remote(piece, piece, gsend.at[0], grecv.at[3], y_up).start()
        remote(above_y, above_y, gsend.at[0], grecv.at[2], y_up).wait_recv()
        piece = gslabs.at[2:4, up]
        remote(piece, piece, gsend.at[0], grecv.at[3], y_dn).start()

    def grad_rotate():
        remote(gslabs.at[:, op], gslabs.at[:, op], gsend.at[0], grecv.at[3], y_up).wait_recv()
        own_ob.wait()

        def rotate(k, carry):
            a = gslabs[k // 2, 2 * (k % 2)].astype(F32)
            b = gslabs[k // 2, 2 * (k % 2) + 1].astype(F32)
            both = jnp.concatenate([a, b], axis=0).astype(BF)
            prod = jnp.dot(both, obas[...], preferred_element_type=F32)
            gpart[0, k] = prod[:, :256]
            gpart[1, k] = prod[:, 256:]
            return carry

        lax.fori_loop(0, 8, rotate, 0)
        gship(16, gpart.at[1 - core], gcore, twin)

    def x_dev(x_):
        return row_dev(x_, zl, core)

    def grad_core():
        glanded(16, gcore, twin)

        def add(k, carry):
            gpart[core, k] = gpart[core, k] + gcore[k]
            return carry

        lax.fori_loop(0, 8, add, 0)
        for o in (1, 2, 3):
            k = (x + o) % 4
            pair = gpart.at[core, pl.ds(2 * k, 2)]
            remote(pair, gin.at[x], gsend.at[17], grecv.at[17], x_dev(k)).start()

    def grad_x():
        glanded(17, gin.at[0:3], x_up)
        for o in (1, 2, 3):
            k = (x + o) % 4
            for i in range(2):
                gpart[core, 2 * x + i] = gpart[core, 2 * x + i] + gin[k, i]
        gship(21, gpart.at[core, 2 * x + zo], gpair, z_pair)

    def grad_sum():
        glanded(21, gpair, z_pair)
        grot[core, 2 * x + zl] = (gpart[core, 2 * x + zl] + gpair[...]).astype(BF)
        piece = grot.at[core, 2 * x + zl]
        gship(22, piece, piece, z_pair)

    def grad_z():
        glanded(22, grot.at[core, 2 * x + zo], z_pair)
        pair = grot.at[core, pl.ds(2 * x, 2)]
        for o in (1, 2, 3):
            k = (x + o) % 4
            remote(pair, pair, gsend.at[23], grecv.at[23], x_dev(k)).start()

    def grad_gather():
        glanded(23, grot.at[core, 0:6], x_up)
        gship(27, grot.at[core], grot.at[core], twin)

    def grad_done():
        glanded(27, grot.at[1 - core], twin)
        for i in range(8):
            k = order[i][1] * 4 + order[i][0]
            rows = labels[pl.ds(pl.multiple_of(k * 144, 16), 144), :]
            for s in range(NSEQ):
                member = (rows == s).astype(F32).astype(BF)
                member = jnp.concatenate([member, member], axis=1)
                for h in range(2):
                    gmask[s, h, pl.ds(i * 144, 144), :] = grot[h, k] * member
        lax.fori_loop(0, (GDONE - LAGS[-1]) // 2 - LEAD, lambda j, carry: (square(j), carry)[1], 0)

    stages = [stage_compute, stage_half, stage_full, stage_z, stage_gather, stage_relay, stage_last]
    deep = LAGS[-1]
    extras = {
        0: act_far, 1: grad_y, 2: act_cross, 4: act_last, 5: grad_relay, 8: grad_rotate, 9: grad_core,
        16: grad_x, 18: grad_sum, 20: grad_z, 24: grad_gather, GDONE: grad_done,
    }

    def turn(pair, carry):
        for parity in range(2):
            now = 2 * pair + parity
            for lag, stage in zip(LAGS, stages):
                m = (parity + lag) % 2
                j = (now - lag - m) // 2 - m * LEAD

                @pl.when((j >= 0) & (j < STEPS))
                def _():
                    stage(j, m)
                    if lag == deep and m == 1:
                        pl.when(now >= GDONE)(lambda: square(j))

            for at, extra in extras.items():
                if at % 2 == parity:
                    pl.when(now == at)(extra)

        return carry

    lax.fori_loop(0, (2 * (STEPS - 1 + LEAD) + 1 + deep) // 2 + 1, turn, 0)

    for j in range(STEPS):
        out_copy(j).wait()

    def sent(sem, ref):
        remote(ref, ref, sem, sem, twin).wait_send()

    sent(send.at[0], half_out)
    sent(send.at[1], full_out)
    sent(send.at[2], z_out.at[:, 0:3])
    sent(send.at[3], z_out.at[:, 0:3])
    sent(send.at[4], rot.at[:, 0:2])
    sent(send.at[5], rot.at[:, 0])
    sent(asend.at[0], slabs.at[0:15])
    sent(gsend.at[0], gslabs.at[0:3])
    sent(gsend.at[0], gslabs.at[0, 0:3])
    sent(gsend.at[16], gcore)
    sent(gsend.at[17], gin.at[0:3])
    sent(gsend.at[21], gpair)
    sent(gsend.at[22], grot.at[core, 0])
    sent(gsend.at[23], grot.at[core, 0:6])
    sent(gsend.at[27], grot.at[core])


def shards(activations, grad_outputs, input_basis, output_basis, segment_ids):
    hbm = pl.BlockSpec(memory_space=pl.ANY)
    dma = pltpu.SemaphoreType.DMA
    return pl.pallas_call(
        kernel,
        out_shape=jax.ShapeDtypeStruct((CIN, GIN), F32),
        in_specs=[hbm, hbm, hbm, hbm, pl.BlockSpec(memory_space=pltpu.VMEM)],
        out_specs=hbm,
        scratch_shapes=[
            pltpu.VMEM((16, SLAB, CIN), BF),
            pltpu.VMEM((TOK, CIN), BF),
            pltpu.VMEM((STEPS, CIN, WIDE), BF),
            pltpu.VMEM((GIN, GIN), BF),
            pltpu.VMEM((STEPS, 4, QUARTER, TOK), F32),
            pltpu.VMEM((STEPS, 2, HALF, TOK), BF),
            pltpu.VMEM((STEPS, 2, HALF, TOK), BF),
            pltpu.VMEM((STEPS, 2, QUARTER, TOK), BF),
            pltpu.VMEM((STEPS, 2, QUARTER, TOK), BF),
            pltpu.VMEM((STEPS, 4, PIECE, TOK), BF),
            pltpu.VMEM((STEPS, 4, PIECE, TOK), BF),
            pltpu.VMEM((STEPS, 4, 4, PIECE, TOK), BF),
            pltpu.VMEM((STEPS, WIDE, GIN), F32),
            pltpu.VMEM((4, 4, SLAB, GIN), BF),
            pltpu.VMEM((2, 8, 144, 256), F32),
            pltpu.VMEM((8, 144, 256), F32),
            pltpu.VMEM((4, 2, 144, 256), F32),
            pltpu.VMEM((144, 256), F32),
            pltpu.VMEM((2, 8, 144, 256), BF),
            pltpu.VMEM((NSEQ, 2, TOK, 256), BF),
            pltpu.VMEM((TOK, 128), F32),
            dma((6,)),
            dma((STEPS, 2, 8)),
            dma((1,)),
            dma((17,)),
            dma((28,)),
            dma((28,)),
            dma((17,)),
        ],
        compiler_params=pltpu.CompilerParams(
            collective_id=0, has_side_effects=True, vmem_limit_bytes=60 * 1024 * 1024
        ),
        cost_estimate=pl.CostEstimate(flops=15_000_000_000, bytes_accessed=16_000_000, transcendentals=0),
    )(activations, grad_outputs, input_basis, output_basis, segment_ids)


def solution(mesh):
    placed = (P("row", "col"), P("col", "row"), P("col", "row"), P("row", "col"), P())
    return jax.shard_map(
        shards, mesh=mesh, in_specs=placed, out_specs=P("row", "col"), check_vma=False
    )
```

```python
import jax
import jax.numpy as jnp
from jax import lax
from jax.experimental import pallas as pl
from jax.experimental.pallas import tpu as pltpu
from jax.sharding import PartitionSpec as P

MESH = pl.DeviceIdType.MESH
NSEQ = 3
TOK = 1152
SLAB = 72
CIN = 1792
GIN = 512
STEPS = 7
WIDE = 256
QUARTER = 64
HALF = 32
PIECE = 16
LANES = ((0, 512), (512, 640))
LEAD = 2
GDONE = 28
LAGS = (0, 2, 4, 7, 10, 12, 14)
BF = jnp.bfloat16
F32 = jnp.float32


def kernel(
    act, grad, basis, obasis, ids, out,
    slabs, acts, bas, obas, part, half_out, half_in, full_out, full_in, z_out, z_in, rot, res,
    gslabs, gpart, gcore, gin, gpair, grot, gmask, labels,
    send, recv, asend, arecv, gsend, grecv, local,
):
    r, c = lax.axis_index("row"), lax.axis_index("col")
    core, x, zl = r % 2, (r // 2) % 4, r // 8
    y, zh = c % 4, c // 4

    def row_dev(x_, zl_, core_):
        return {"row": zl_ * 8 + x_ * 2 + core_, "col": c}

    def col_dev(y_, zh_):
        return {"row": r, "col": zh_ * 4 + y_}

    twin = row_dev(x, zl, 1 - core)
    x_up, x_dn = row_dev((x + 1) % 4, zl, core), row_dev((x + 3) % 4, zl, core)
    z_pair = row_dev(x, 1 - zl, core)
    y_up, y_dn = col_dev((y + 1) % 4, zh), col_dev((y + 3) % 4, zh)

    x_far = row_dev((x + 2) % 4, zl, core)

    barrier = pltpu.get_barrier_semaphore()
    for dev in [twin, x_up, x_dn, z_pair, x_far, y_up, y_dn] + [col_dev(y, (zh + o) % 4) for o in (1, 2, 3)]:
        pl.semaphore_signal(barrier, inc=1, device_id=dev, device_id_type=MESH)
    pl.semaphore_wait(barrier, 10)

    def remote(src, dst, s, d, dev):
        return pltpu.make_async_remote_copy(
            src_ref=src, dst_ref=dst, send_sem=s, recv_sem=d, device_id=dev, device_id_type=MESH
        )

    own_act = pltpu.make_async_copy(act, slabs.at[r], local.at[0])
    own_grad = pltpu.make_async_copy(grad, gslabs.at[zh, y], local.at[1])
    own_act.start()
    own_grad.start()
    own_ob = pltpu.make_async_copy(obasis, obas, local.at[2])
    own_ob.start()

    def basis_copy(j):
        return pltpu.make_async_copy(
            basis.at[:, pl.ds(pl.multiple_of(j * WIDE, WIDE), WIDE)], bas.at[j], local.at[3 + j]
        )

    def slab_at(x_, zl_, core_):
        return slabs.at[zl_ * 8 + x_ * 2 + core_]

    LO, HI = slice(0, CIN // 2), slice(CIN // 2, CIN)

    def ship(n, src, dst, dev):
        d = remote(src, dst, asend.at[0], arecv.at[n], dev)
        d.start()

    def landed(n, dst, dev):
        remote(dst, dst, asend.at[0], arecv.at[n], dev).wait_recv()

    xm, xp, xo, zo = (x + 3) % 4, (x + 1) % 4, (x + 2) % 4, 1 - zl
    mine = slabs.at[r]

    ship(0, act, mine, z_pair)
    ship(1, act, mine, x_up)
    ship(2, act, mine, x_dn)
    ship(9, act, mine, twin)

    def gship(n, src, dst, dev):
        remote(src, dst, gsend.at[n], grecv.at[n], dev).start()

    def glanded(n, dst, dev):
        remote(dst, dst, gsend.at[n], grecv.at[n], dev).wait_recv()

    for j in range(STEPS):
        basis_copy(j).start()

    below, above, far = slab_at(xm, zl, core), slab_at(xp, zl, core), slab_at(xo, zl, core)
    landed(1, below, x_dn)
    ship(5, below.at[:, LO], below.at[:, LO], x_up)
    ship(11, below, below, twin)
    landed(2, above, x_up)
    ship(6, above.at[:, HI], above.at[:, HI], x_dn)
    ship(12, above, above, twin)

    landed(0, slab_at(x, zo, core), z_pair)
    ship(3, slab_at(x, zo, core), slab_at(x, zo, core), x_up)
    ship(4, slab_at(x, zo, core), slab_at(x, zo, core), x_dn)
    ship(10, slab_at(x, zo, core), slab_at(x, zo, core), twin)

    for o in (1, 2, 3):
        h = (zh + o) % 4
        remote(grad, gslabs.at[zh, y], gsend.at[0], grecv.at[0], col_dev(y, h)).start()

    order = ((x, zl), (x, zo), (xm, zl), (xp, zl), (xo, zl), (xm, zo), (xp, zo), (xo, zo))

    def join(i):
        k = order[i][1] * 4 + order[i][0]
        a = slabs[2 * k].astype(F32)
        b = slabs[2 * k + 1].astype(F32)
        acts[pl.ds(i * 144, 144), :] = jnp.concatenate([a, b], axis=0).astype(BF)

    own_act.wait()
    for n, i in ((9, 0), (10, 1), (11, 2), (12, 3)):
        landed(n, slab_at(*order[i], 1 - core), twin)
        join(i)

    def act_far():
        landed(5, far.at[:, LO], x_dn)
        landed(6, far.at[:, HI], x_up)
        ship(7, far, far, z_pair)
        ship(15, far, far, twin)

    def act_cross():
        for n, x_, dev, out_n in ((3, xm, x_dn, 13), (4, xp, x_up, 14)):
            landed(n, slab_at(x_, zo, core), dev)
            ship(out_n, slab_at(x_, zo, core), slab_at(x_, zo, core), twin)

    def act_last():
        landed(7, slab_at(xo, zo, core), z_pair)
        ship(16, slab_at(xo, zo, core), slab_at(xo, zo, core), twin)
        for n, i in ((15, 4), (13, 5), (14, 6), (16, 7)):
            landed(n, slab_at(*order[i], 1 - core), twin)
            join(i)

    label = ids[...].reshape(1, TOK)
    weights = [
        1.0 / (jnp.sum((label == s).astype(F32), axis=1, keepdims=True) * NSEQ) for s in range(NSEQ)
    ]
    labels[...] = jnp.broadcast_to(label.astype(F32), (128, TOK)).T

    up, dn, op = (y + 1) % 4, (y + 3) % 4, (y + 2) % 4
    others = [(zh + o) % 4 for o in (1, 2, 3)]

    def msg(j, m, n_send, n_recv, src, dst, dev):
        return remote(src, dst, send.at[n_send], recv.at[j, m, n_recv], dev)

    def lanes(m):
        return pl.ds(*LANES[m])

    def stage_compute(j, m):
        ln = lanes(m)
        if m == 0:
            basis_copy(j).wait()
        prod = jnp.dot(acts[ln, :], bas[j], preferred_element_type=F32)
        part[j, :, :, ln] = prod.T.reshape(4, QUARTER, LANES[m][1])
        half_out[j, 0, :, ln] = part[j, op, :HALF, ln].astype(BF)
        half_out[j, 1, :, ln] = part[j, op, HALF:, ln].astype(BF)
        for n, dev in ((0, y_up), (1, y_dn)):
            msg(j, m, 0, n, half_out.at[j, n, :, ln], half_in.at[j, n, :, ln], dev).start()

    def stage_half(j, m):
        ln = lanes(m)
        msg(j, m, 0, 0, half_out.at[j, 0, :, ln], half_in.at[j, 0, :, ln], y_dn).wait_recv()
        full_out[j, 0, :HALF, ln] = (part[j, up, :HALF, ln] + half_in[j, 0, :, ln].astype(F32)).astype(BF)
        full_out[j, 0, HALF:, ln] = part[j, up, HALF:, ln].astype(BF)
        msg(j, m, 1, 2, full_out.at[j, 0, :, ln], full_in.at[j, 0, :, ln], y_up).start()
        msg(j, m, 0, 1, half_out.at[j, 1, :, ln], half_in.at[j, 1, :, ln], y_up).wait_recv()
        full_out[j, 1, HALF:, ln] = (part[j, dn, HALF:, ln] + half_in[j, 1, :, ln].astype(F32)).astype(BF)
        full_out[j, 1, :HALF, ln] = part[j, dn, :HALF, ln].astype(BF)
        msg(j, m, 1, 2, full_out.at[j, 1, :, ln], full_in.at[j, 1, :, ln], y_dn).start()

    def stage_full(j, m):
        ln = lanes(m)
        msg(j, m, 1, 2, full_out.at[j, :, :, ln], full_in.at[j, :, :, ln], y_dn).wait_recv()
        total = part[j, y, :, ln] + full_in[j, 0, :, ln].astype(F32) + full_in[j, 1, :, ln].astype(F32)
        part[j, y, :, ln] = total
        z_out[j, :, :, ln] = total.astype(BF).reshape(4, PIECE, LANES[m][1])
        for h in others:
            msg(j, m, 2, 3, z_out.at[j, h, :, ln], z_in.at[j, zh, :, ln], col_dev(y, h)).start()

    def stage_z(j, m):
        ln = lanes(m)
        total = part[j, y, pl.ds(pl.multiple_of(zh * PIECE, PIECE), PIECE), ln]
        msg(j, m, 2, 3, z_out.at[j, 0:3, :, ln], z_in.at[j, 0:3, :, ln], y_up).wait_recv()
        for h in others:
            total = total + z_in[j, h, :, ln].astype(F32)
        rot[j, y, zh, :, ln] = total.astype(BF)
        piece = rot.at[j, y, zh, :, ln]
        for h in others:
            msg(j, m, 3, 4, piece, piece, col_dev(y, h)).start()

    def stage_gather(j, m):
        ln = lanes(m)
        pieces = rot.at[j, y, 0:3, :, ln]
        msg(j, m, 3, 4, pieces, pieces, y_up).wait_recv()
        quarter = rot.at[j, y, :, :, ln]
        msg(j, m, 4, 5, quarter, quarter, y_up).start()
        msg(j, m, 4, 6, quarter, quarter, y_dn).start()

    def stage_relay(j, m):
        ln = lanes(m)
        below, above = rot.at[j, dn, :, :, ln], rot.at[j, up, :, :, ln]
        msg(j, m, 4, 5, below, below, y_dn).wait_recv()
        piece = rot.at[j, dn, 0:2, :, ln]
        msg(j, m, 5, 7, piece, piece, y_up).start()
        msg(j, m, 4, 6, above, above, y_up).wait_recv()
        piece = rot.at[j, up, 2:4, :, ln]
        msg(j, m, 5, 7, piece, piece, y_dn).start()

    def stage_last(j, m):
        ln = lanes(m)
        quarter = rot.at[j, op, :, :, ln]
        msg(j, m, 5, 7, quarter, quarter, y_dn).wait_recv()

    def out_copy(j):
        return pltpu.make_async_copy(
            res.at[j], out.at[pl.ds(pl.multiple_of(j * WIDE, WIDE), WIDE), :], local.at[10 + j]
        )

    def square(j):
        a = rot[j].reshape(WIDE, TOK)
        for h in range(2):
            total = None
            for s in range(NSEQ):
                p = jnp.dot(a, gmask[s, h], preferred_element_type=F32)
                term = p * p * weights[s]
                total = term if total is None else total + term
            res[j, :, pl.ds(h * 256, 256)] = total
        out_copy(j).start()

    def grad_y():
        own_grad.wait()
        remote(gslabs.at[0:3, 0], gslabs.at[0:3, 0], gsend.at[0], grecv.at[0], y_up).wait_recv()
        mine_y = gslabs.at[:, y]
        remote(mine_y, mine_y, gsend.at[0], grecv.at[1], y_up).start()
        remote(mine_y, mine_y, gsend.at[0], grecv.at[2], y_dn).start()

    def grad_relay():
        below_y, above_y = gslabs.at[:, dn], gslabs.at[:, up]
        remote(below_y, below_y, gsend.at[0], grecv.at[1], y_dn).wait_recv()
        piece = gslabs.at[0:2, dn]
        remote(piece, piece, gsend.at[0], grecv.at[3], y_up).start()
        remote(above_y, above_y, gsend.at[0], grecv.at[2], y_up).wait_recv()
        piece = gslabs.at[2:4, up]
        remote(piece, piece, gsend.at[0], grecv.at[3], y_dn).start()

    def grad_rotate():
        remote(gslabs.at[:, op], gslabs.at[:, op], gsend.at[0], grecv.at[3], y_up).wait_recv()
        own_ob.wait()

        def rotate(k, carry):
            a = gslabs[k // 2, 2 * (k % 2)].astype(F32)
            b = gslabs[k // 2, 2 * (k % 2) + 1].astype(F32)
            both = jnp.concatenate([a, b], axis=0).astype(BF)
            prod = jnp.dot(both, obas[...], preferred_element_type=F32)
            gpart[0, k] = prod[:, :256]
            gpart[1, k] = prod[:, 256:]
            return carry

        lax.fori_loop(0, 8, rotate, 0)
        gship(16, gpart.at[1 - core], gcore, twin)

    def x_dev(x_):
        return row_dev(x_, zl, core)

    def grad_core():
        glanded(16, gcore, twin)

        def add(k, carry):
            gpart[core, k] = gpart[core, k] + gcore[k]
            return carry

        lax.fori_loop(0, 8, add, 0)
        for o in (1, 2, 3):
            k = (x + o) % 4
            pair = gpart.at[core, pl.ds(2 * k, 2)]
            remote(pair, gin.at[x], gsend.at[17], grecv.at[17], x_dev(k)).start()

    def grad_x():
        glanded(17, gin.at[0:3], x_up)
        for o in (1, 2, 3):
            k = (x + o) % 4
            for i in range(2):
                gpart[core, 2 * x + i] = gpart[core, 2 * x + i] + gin[k, i]
        gship(21, gpart.at[core, 2 * x + zo], gpair, z_pair)

    def grad_sum():
        glanded(21, gpair, z_pair)
        grot[core, 2 * x + zl] = (gpart[core, 2 * x + zl] + gpair[...]).astype(BF)
        piece = grot.at[core, 2 * x + zl]
        gship(22, piece, piece, z_pair)

    def grad_z():
        glanded(22, grot.at[core, 2 * x + zo], z_pair)
        pair = grot.at[core, pl.ds(2 * x, 2)]
        for o in (1, 2, 3):
            k = (x + o) % 4
            remote(pair, pair, gsend.at[23], grecv.at[23], x_dev(k)).start()

    def grad_gather():
        glanded(23, grot.at[core, 0:6], x_up)
        gship(27, grot.at[core], grot.at[core], twin)

    def grad_done():
        glanded(27, grot.at[1 - core], twin)
        for i in range(8):
            k = order[i][1] * 4 + order[i][0]
            rows = labels[pl.ds(pl.multiple_of(k * 144, 16), 144), :]
            for s in range(NSEQ):
                member = (rows == s).astype(F32).astype(BF)
                member = jnp.concatenate([member, member], axis=1)
                for h in range(2):
                    gmask[s, h, pl.ds(i * 144, 144), :] = grot[h, k] * member
        lax.fori_loop(0, (GDONE - LAGS[-1]) // 2 - LEAD, lambda j, carry: (square(j), carry)[1], 0)

    stages = [stage_compute, stage_half, stage_full, stage_z, stage_gather, stage_relay, stage_last]
    deep = LAGS[-1]
    extras = (
        (1, act_far), (3, grad_y), (4, act_cross), (4, act_last), (7, grad_relay), (10, grad_rotate), (11, grad_core), (18, grad_x), (20, grad_sum), (22, grad_z), (25, grad_gather), (GDONE, grad_done),
    )

    def turn(pair, carry):
        for parity in range(2):
            now = 2 * pair + parity
            for lag, stage in zip(LAGS, stages):
                m = (parity + lag) % 2
                j = (now - lag - m) // 2 - m * LEAD

                @pl.when((j >= 0) & (j < STEPS))
                def _():
                    stage(j, m)
                    if lag == deep and m == 1:
                        pl.when(now >= GDONE)(lambda: square(j))

            for at, extra in extras:
                if at % 2 == parity:
                    pl.when(now == at)(extra)

        return carry

    lax.fori_loop(0, (2 * (STEPS - 1 + LEAD) + 1 + deep) // 2 + 1, turn, 0)

    for j in range(STEPS):
        out_copy(j).wait()

    def sent(sem, ref):
        remote(ref, ref, sem, sem, twin).wait_send()

    sent(send.at[0], half_out)
    sent(send.at[1], full_out)
    sent(send.at[2], z_out.at[:, 0:3])
    sent(send.at[3], z_out.at[:, 0:3])
    sent(send.at[4], rot.at[:, 0:2])
    sent(send.at[5], rot.at[:, 0])
    sent(asend.at[0], slabs.at[0:15])
    sent(gsend.at[0], gslabs.at[0:3])
    sent(gsend.at[0], gslabs.at[0, 0:3])
    sent(gsend.at[16], gcore)
    sent(gsend.at[17], gin.at[0:3])
    sent(gsend.at[21], gpair)
    sent(gsend.at[22], grot.at[core, 0])
    sent(gsend.at[23], grot.at[core, 0:6])
    sent(gsend.at[27], grot.at[core])


def shards(activations, grad_outputs, input_basis, output_basis, segment_ids):
    hbm = pl.BlockSpec(memory_space=pl.ANY)
    dma = pltpu.SemaphoreType.DMA
    return pl.pallas_call(
        kernel,
        out_shape=jax.ShapeDtypeStruct((CIN, GIN), F32),
        in_specs=[hbm, hbm, hbm, hbm, pl.BlockSpec(memory_space=pltpu.VMEM)],
        out_specs=hbm,
        scratch_shapes=[
            pltpu.VMEM((16, SLAB, CIN), BF),
            pltpu.VMEM((TOK, CIN), BF),
            pltpu.VMEM((STEPS, CIN, WIDE), BF),
            pltpu.VMEM((GIN, GIN), BF),
            pltpu.VMEM((STEPS, 4, QUARTER, TOK), F32),
            pltpu.VMEM((STEPS, 2, HALF, TOK), BF),
            pltpu.VMEM((STEPS, 2, HALF, TOK), BF),
            pltpu.VMEM((STEPS, 2, QUARTER, TOK), BF),
            pltpu.VMEM((STEPS, 2, QUARTER, TOK), BF),
            pltpu.VMEM((STEPS, 4, PIECE, TOK), BF),
            pltpu.VMEM((STEPS, 4, PIECE, TOK), BF),
            pltpu.VMEM((STEPS, 4, 4, PIECE, TOK), BF),
            pltpu.VMEM((STEPS, WIDE, GIN), F32),
            pltpu.VMEM((4, 4, SLAB, GIN), BF),
            pltpu.VMEM((2, 8, 144, 256), F32),
            pltpu.VMEM((8, 144, 256), F32),
            pltpu.VMEM((4, 2, 144, 256), F32),
            pltpu.VMEM((144, 256), F32),
            pltpu.VMEM((2, 8, 144, 256), BF),
            pltpu.VMEM((NSEQ, 2, TOK, 256), BF),
            pltpu.VMEM((TOK, 128), F32),
            dma((6,)),
            dma((STEPS, 2, 8)),
            dma((1,)),
            dma((17,)),
            dma((28,)),
            dma((28,)),
            dma((17,)),
        ],
        compiler_params=pltpu.CompilerParams(
            collective_id=0, has_side_effects=True, vmem_limit_bytes=60 * 1024 * 1024
        ),
        cost_estimate=pl.CostEstimate(flops=15_000_000_000, bytes_accessed=16_000_000, transcendentals=0),
    )(activations, grad_outputs, input_basis, output_basis, segment_ids)


def solution(mesh):
    placed = (P("row", "col"), P("col", "row"), P("col", "row"), P("row", "col"), P())
    return jax.shard_map(
        shards, mesh=mesh, in_specs=placed, out_specs=P("row", "col"), check_vma=False
    )
```

```python
import jax
import jax.numpy as jnp
from jax import lax
from jax.experimental import pallas as pl
from jax.experimental.pallas import tpu as pltpu
from jax.sharding import PartitionSpec as P

MESH = pl.DeviceIdType.MESH
NSEQ = 3
TOK = 1152
SLAB = 72
CIN = 1792
GIN = 512
STEPS = 7
WIDE = 256
QUARTER = 64
HALF = 32
PIECE = 16
LANES = ((0, 512), (512, 640))
LEAD = 1
GDONE = 24
LAGS = ((0, 2, 4, 6, 8, 10, 12), (0, 2, 4, 6, 8, 10, 12))
BF = jnp.bfloat16
F32 = jnp.float32


def kernel(
    act, grad, basis, obasis, ids, out,
    slabs, acts, bas, obas, part, half_out, half_in, full_out, full_in, z_out, z_in, rot, res,
    gslabs, gpart, gcore, gin, gpair, grot, gmask, labels,
    send, recv, asend, arecv, gsend, grecv, local,
):
    r, c = lax.axis_index("row"), lax.axis_index("col")
    core, x, zl = r % 2, (r // 2) % 4, r // 8
    y, zh = c % 4, c // 4

    def row_dev(x_, zl_, core_):
        return {"row": zl_ * 8 + x_ * 2 + core_, "col": c}

    def col_dev(y_, zh_):
        return {"row": r, "col": zh_ * 4 + y_}

    twin = row_dev(x, zl, 1 - core)
    x_up, x_dn = row_dev((x + 1) % 4, zl, core), row_dev((x + 3) % 4, zl, core)
    z_pair = row_dev(x, 1 - zl, core)
    y_up, y_dn = col_dev((y + 1) % 4, zh), col_dev((y + 3) % 4, zh)

    x_far = row_dev((x + 2) % 4, zl, core)

    barrier = pltpu.get_barrier_semaphore()
    for dev in [twin, x_up, x_dn, z_pair, x_far, y_up, y_dn] + [col_dev(y, (zh + o) % 4) for o in (1, 2, 3)]:
        pl.semaphore_signal(barrier, inc=1, device_id=dev, device_id_type=MESH)
    pl.semaphore_wait(barrier, 10)

    def remote(src, dst, s, d, dev):
        return pltpu.make_async_remote_copy(
            src_ref=src, dst_ref=dst, send_sem=s, recv_sem=d, device_id=dev, device_id_type=MESH
        )

    own_act = pltpu.make_async_copy(act, slabs.at[r], local.at[0])
    own_grad = pltpu.make_async_copy(grad, gslabs.at[zh, y], local.at[1])
    own_act.start()
    own_grad.start()
    own_ob = pltpu.make_async_copy(obasis, obas, local.at[2])
    own_ob.start()

    def basis_copy(j):
        return pltpu.make_async_copy(
            basis.at[:, pl.ds(pl.multiple_of(j * WIDE, WIDE), WIDE)], bas.at[j], local.at[3 + j]
        )

    def slab_at(x_, zl_, core_):
        return slabs.at[zl_ * 8 + x_ * 2 + core_]

    LO, HI = slice(0, CIN // 2), slice(CIN // 2, CIN)

    def ship(n, src, dst, dev):
        d = remote(src, dst, asend.at[0], arecv.at[n], dev)
        d.start()

    def landed(n, dst, dev):
        remote(dst, dst, asend.at[0], arecv.at[n], dev).wait_recv()

    xm, xp, xo, zo = (x + 3) % 4, (x + 1) % 4, (x + 2) % 4, 1 - zl
    mine = slabs.at[r]

    ship(0, act, mine, z_pair)
    ship(1, act.at[:, LO], mine.at[:, LO], x_up)
    ship(2, act.at[:, HI], mine.at[:, HI], x_dn)
    ship(17, act.at[:, HI], mine.at[:, HI], x_up)
    ship(18, act.at[:, LO], mine.at[:, LO], x_dn)
    ship(9, act, mine, twin)

    def gship(n, src, dst, dev):
        remote(src, dst, gsend.at[n], grecv.at[n], dev).start()

    def glanded(n, dst, dev):
        remote(dst, dst, gsend.at[n], grecv.at[n], dev).wait_recv()

    for j in range(STEPS):
        basis_copy(j).start()

    below, above, far = slab_at(xm, zl, core), slab_at(xp, zl, core), slab_at(xo, zl, core)
    landed(1, below.at[:, LO], x_dn)
    ship(5, below.at[:, LO], below.at[:, LO], x_up)
    landed(2, above.at[:, HI], x_up)
    ship(6, above.at[:, HI], above.at[:, HI], x_dn)
    landed(17, below.at[:, HI], x_dn)
    ship(11, below, below, twin)
    landed(18, above.at[:, LO], x_up)
    ship(12, above, above, twin)

    landed(0, slab_at(x, zo, core), z_pair)
    ship(3, slab_at(x, zo, core), slab_at(x, zo, core), x_up)
    ship(4, slab_at(x, zo, core), slab_at(x, zo, core), x_dn)
    ship(10, slab_at(x, zo, core), slab_at(x, zo, core), twin)

    for o in (1, 2, 3):
        h = (zh + o) % 4
        remote(grad, gslabs.at[zh, y], gsend.at[0], grecv.at[0], col_dev(y, h)).start()

    order = ((x, zl), (x, zo), (xm, zl), (xp, zl), (xo, zl), (xm, zo), (xp, zo), (xo, zo))

    def join(i):
        k = order[i][1] * 4 + order[i][0]
        a = slabs[2 * k].astype(F32)
        b = slabs[2 * k + 1].astype(F32)
        acts[pl.ds(i * 144, 144), :] = jnp.concatenate([a, b], axis=0).astype(BF)

    own_act.wait()
    for n, i in ((9, 0), (10, 1), (11, 2), (12, 3)):
        landed(n, slab_at(*order[i], 1 - core), twin)
        join(i)

    def act_far():
        landed(5, far.at[:, LO], x_dn)
        landed(6, far.at[:, HI], x_up)
        ship(7, far, far, z_pair)
        ship(15, far, far, twin)

    def act_cross():
        for n, x_, dev, out_n in ((3, xm, x_dn, 13), (4, xp, x_up, 14)):
            landed(n, slab_at(x_, zo, core), dev)
            ship(out_n, slab_at(x_, zo, core), slab_at(x_, zo, core), twin)

    def act_last():
        landed(7, slab_at(xo, zo, core), z_pair)
        ship(16, slab_at(xo, zo, core), slab_at(xo, zo, core), twin)
        for n, i in ((15, 4), (13, 5), (14, 6), (16, 7)):
            landed(n, slab_at(*order[i], 1 - core), twin)
            join(i)

    label = ids[...].reshape(1, TOK)
    weights = [
        1.0 / (jnp.sum((label == s).astype(F32), axis=1, keepdims=True) * NSEQ) for s in range(NSEQ)
    ]
    labels[...] = jnp.broadcast_to(label.astype(F32), (128, TOK)).T

    up, dn, op = (y + 1) % 4, (y + 3) % 4, (y + 2) % 4
    others = [(zh + o) % 4 for o in (1, 2, 3)]

    def msg(j, m, n_send, n_recv, src, dst, dev):
        return remote(src, dst, send.at[n_send], recv.at[j, m, n_recv], dev)

    def lanes(m):
        return pl.ds(*LANES[m])

    def stage_compute(j, m):
        ln = lanes(m)
        if m == 0:
            basis_copy(j).wait()
        prod = jnp.dot(acts[ln, :], bas[j], preferred_element_type=F32)
        part[j, :, :, ln] = prod.T.reshape(4, QUARTER, LANES[m][1])
        half_out[j, 0, :, ln] = part[j, op, :HALF, ln].astype(BF)
        half_out[j, 1, :, ln] = part[j, op, HALF:, ln].astype(BF)
        for n, dev in ((0, y_up), (1, y_dn)):
            msg(j, m, 0, n, half_out.at[j, n, :, ln], half_in.at[j, n, :, ln], dev).start()

    def stage_half(j, m):
        ln = lanes(m)
        msg(j, m, 0, 0, half_out.at[j, 0, :, ln], half_in.at[j, 0, :, ln], y_dn).wait_recv()
        full_out[j, 0, :HALF, ln] = (part[j, up, :HALF, ln] + half_in[j, 0, :, ln].astype(F32)).astype(BF)
        full_out[j, 0, HALF:, ln] = part[j, up, HALF:, ln].astype(BF)
        msg(j, m, 1, 2, full_out.at[j, 0, :, ln], full_in.at[j, 0, :, ln], y_up).start()
        msg(j, m, 0, 1, half_out.at[j, 1, :, ln], half_in.at[j, 1, :, ln], y_up).wait_recv()
        full_out[j, 1, HALF:, ln] = (part[j, dn, HALF:, ln] + half_in[j, 1, :, ln].astype(F32)).astype(BF)
        full_out[j, 1, :HALF, ln] = part[j, dn, :HALF, ln].astype(BF)
        msg(j, m, 1, 2, full_out.at[j, 1, :, ln], full_in.at[j, 1, :, ln], y_dn).start()

    def stage_full(j, m):
        ln = lanes(m)
        msg(j, m, 1, 2, full_out.at[j, :, :, ln], full_in.at[j, :, :, ln], y_dn).wait_recv()
        total = part[j, y, :, ln] + full_in[j, 0, :, ln].astype(F32) + full_in[j, 1, :, ln].astype(F32)
        part[j, y, :, ln] = total
        z_out[j, :, :, ln] = total.astype(BF).reshape(4, PIECE, LANES[m][1])
        for h in others:
            msg(j, m, 2, 3, z_out.at[j, h, :, ln], z_in.at[j, zh, :, ln], col_dev(y, h)).start()

    def stage_z(j, m):
        ln = lanes(m)
        total = part[j, y, pl.ds(pl.multiple_of(zh * PIECE, PIECE), PIECE), ln]
        msg(j, m, 2, 3, z_out.at[j, 0:3, :, ln], z_in.at[j, 0:3, :, ln], y_up).wait_recv()
        for h in others:
            total = total + z_in[j, h, :, ln].astype(F32)
        rot[j, y, zh, :, ln] = total.astype(BF)
        piece = rot.at[j, y, zh, :, ln]
        for h in others:
            msg(j, m, 3, 4, piece, piece, col_dev(y, h)).start()

    def stage_gather(j, m):
        ln = lanes(m)
        pieces = rot.at[j, y, 0:3, :, ln]
        msg(j, m, 3, 4, pieces, pieces, y_up).wait_recv()
        quarter = rot.at[j, y, :, :, ln]
        msg(j, m, 4, 5, quarter, quarter, y_up).start()
        msg(j, m, 4, 6, quarter, quarter, y_dn).start()

    def stage_relay(j, m):
        ln = lanes(m)
        below, above = rot.at[j, dn, :, :, ln], rot.at[j, up, :, :, ln]
        msg(j, m, 4, 5, below, below, y_dn).wait_recv()
        piece = rot.at[j, dn, 0:2, :, ln]
        msg(j, m, 5, 7, piece, piece, y_up).start()
        msg(j, m, 4, 6, above, above, y_up).wait_recv()
        piece = rot.at[j, up, 2:4, :, ln]
        msg(j, m, 5, 7, piece, piece, y_dn).start()

    def stage_last(j, m):
        ln = lanes(m)
        quarter = rot.at[j, op, :, :, ln]
        msg(j, m, 5, 7, quarter, quarter, y_dn).wait_recv()

    def out_copy(j):
        return pltpu.make_async_copy(
            res.at[j], out.at[pl.ds(pl.multiple_of(j * WIDE, WIDE), WIDE), :], local.at[10 + j]
        )

    def square(j):
        a = rot[j].reshape(WIDE, TOK)
        for h in range(2):
            total = None
            for s in range(NSEQ):
                p = jnp.dot(a, gmask[s, h], preferred_element_type=F32)
                term = p * p * weights[s]
                total = term if total is None else total + term
            res[j, :, pl.ds(h * 256, 256)] = total
        out_copy(j).start()

    def grad_y():
        own_grad.wait()
        remote(gslabs.at[0:3, 0], gslabs.at[0:3, 0], gsend.at[0], grecv.at[0], y_up).wait_recv()
        mine_y = gslabs.at[:, y]
        remote(mine_y, mine_y, gsend.at[0], grecv.at[1], y_up).start()
        remote(mine_y, mine_y, gsend.at[0], grecv.at[2], y_dn).start()

    def grad_relay():
        below_y, above_y = gslabs.at[:, dn], gslabs.at[:, up]
        remote(below_y, below_y, gsend.at[0], grecv.at[1], y_dn).wait_recv()
        piece = gslabs.at[0:2, dn]
        remote(piece, piece, gsend.at[0], grecv.at[3], y_up).start()
        remote(above_y, above_y, gsend.at[0], grecv.at[2], y_up).wait_recv()
        piece = gslabs.at[2:4, up]
        remote(piece, piece, gsend.at[0], grecv.at[3], y_dn).start()

    def grad_rotate():
        remote(gslabs.at[:, op], gslabs.at[:, op], gsend.at[0], grecv.at[3], y_up).wait_recv()
        own_ob.wait()

        def rotate(k, carry):
            a = gslabs[k // 2, 2 * (k % 2)].astype(F32)
            b = gslabs[k // 2, 2 * (k % 2) + 1].astype(F32)
            both = jnp.concatenate([a, b], axis=0).astype(BF)
            prod = jnp.dot(both, obas[...], preferred_element_type=F32)
            gpart[0, k] = prod[:, :256]
            gpart[1, k] = prod[:, 256:]
            return carry

        lax.fori_loop(0, 8, rotate, 0)
        gship(16, gpart.at[1 - core], gcore, twin)

    def x_dev(x_):
        return row_dev(x_, zl, core)

    def grad_core():
        glanded(16, gcore, twin)

        def add(k, carry):
            gpart[core, k] = gpart[core, k] + gcore[k]
            return carry

        lax.fori_loop(0, 8, add, 0)
        for o in (1, 2, 3):
            k = (x + o) % 4
            pair = gpart.at[core, pl.ds(2 * k, 2)]
            remote(pair, gin.at[x], gsend.at[17], grecv.at[17], x_dev(k)).start()

    def grad_x():
        glanded(17, gin.at[0:3], x_up)
        for o in (1, 2, 3):
            k = (x + o) % 4
            for i in range(2):
                gpart[core, 2 * x + i] = gpart[core, 2 * x + i] + gin[k, i]
        gship(21, gpart.at[core, 2 * x + zo], gpair, z_pair)

    def grad_sum():
        glanded(21, gpair, z_pair)
        grot[core, 2 * x + zl] = (gpart[core, 2 * x + zl] + gpair[...]).astype(BF)
        piece = grot.at[core, 2 * x + zl]
        gship(22, piece, piece, z_pair)

    def grad_z():
        glanded(22, grot.at[core, 2 * x + zo], z_pair)
        pair = grot.at[core, pl.ds(2 * x, 2)]
        for o in (1, 2, 3):
            k = (x + o) % 4
            remote(pair, pair, gsend.at[23], grecv.at[23], x_dev(k)).start()

    def grad_gather():
        glanded(23, grot.at[core, 0:6], x_up)
        gship(27, grot.at[core], grot.at[core], twin)

    def grad_done():
        glanded(27, grot.at[1 - core], twin)
        for i in range(8):
            k = order[i][1] * 4 + order[i][0]
            rows = labels[pl.ds(pl.multiple_of(k * 144, 16), 144), :]
            for s in range(NSEQ):
                member = (rows == s).astype(F32).astype(BF)
                member = jnp.concatenate([member, member], axis=1)
                for h in range(2):
                    gmask[s, h, pl.ds(i * 144, 144), :] = grot[h, k] * member
        lax.fori_loop(0, (GDONE - LAGS[1][-1]) // 2 - LEAD, lambda j, carry: (square(j), carry)[1], 0)

    stages = [stage_compute, stage_half, stage_full, stage_z, stage_gather, stage_relay, stage_last]
    deep = LAGS[1][-1]
    extras = (
        (0, act_far), (2, grad_y), (2, act_cross), (2, act_last), (5, grad_relay), (8, grad_rotate), (9, grad_core), (14, grad_x), (16, grad_sum), (18, grad_z), (21, grad_gather), (GDONE, grad_done),
    )

    def turn(pair, carry):
        for parity in range(2):
            now = 2 * pair + parity
            for k, stage in enumerate(stages):
                for m in range(2):
                    lag = LAGS[m][k]
                    if (parity + lag + m) % 2:
                        continue
                    j = (now - lag - m) // 2 - m * LEAD

                    @pl.when((j >= 0) & (j < STEPS))
                    def _():
                        stage(j, m)
                        if k == len(stages) - 1 and m == 1:
                            pl.when(now >= GDONE)(lambda: square(j))

            for at, extra in extras:
                if at % 2 == parity:
                    pl.when(now == at)(extra)

        return carry

    lax.fori_loop(0, (2 * (STEPS - 1 + LEAD) + 1 + deep) // 2 + 1, turn, 0)

    for j in range(STEPS):
        out_copy(j).wait()

    def sent(sem, ref):
        remote(ref, ref, sem, sem, twin).wait_send()

    sent(send.at[0], half_out)
    sent(send.at[1], full_out)
    sent(send.at[2], z_out.at[:, 0:3])
    sent(send.at[3], z_out.at[:, 0:3])
    sent(send.at[4], rot.at[:, 0:2])
    sent(send.at[5], rot.at[:, 0])
    sent(asend.at[0], slabs.at[0:15])
    sent(gsend.at[0], gslabs.at[0:3])
    sent(gsend.at[0], gslabs.at[0, 0:3])
    sent(gsend.at[16], gcore)
    sent(gsend.at[17], gin.at[0:3])
    sent(gsend.at[21], gpair)
    sent(gsend.at[22], grot.at[core, 0])
    sent(gsend.at[23], grot.at[core, 0:6])
    sent(gsend.at[27], grot.at[core])


def shards(activations, grad_outputs, input_basis, output_basis, segment_ids):
    hbm = pl.BlockSpec(memory_space=pl.ANY)
    dma = pltpu.SemaphoreType.DMA
    return pl.pallas_call(
        kernel,
        out_shape=jax.ShapeDtypeStruct((CIN, GIN), F32),
        in_specs=[hbm, hbm, hbm, hbm, pl.BlockSpec(memory_space=pltpu.VMEM)],
        out_specs=hbm,
        scratch_shapes=[
            pltpu.VMEM((16, SLAB, CIN), BF),
            pltpu.VMEM((TOK, CIN), BF),
            pltpu.VMEM((STEPS, CIN, WIDE), BF),
            pltpu.VMEM((GIN, GIN), BF),
            pltpu.VMEM((STEPS, 4, QUARTER, TOK), F32),
            pltpu.VMEM((STEPS, 2, HALF, TOK), BF),
            pltpu.VMEM((STEPS, 2, HALF, TOK), BF),
            pltpu.VMEM((STEPS, 2, QUARTER, TOK), BF),
            pltpu.VMEM((STEPS, 2, QUARTER, TOK), BF),
            pltpu.VMEM((STEPS, 4, PIECE, TOK), BF),
            pltpu.VMEM((STEPS, 4, PIECE, TOK), BF),
            pltpu.VMEM((STEPS, 4, 4, PIECE, TOK), BF),
            pltpu.VMEM((STEPS, WIDE, GIN), F32),
            pltpu.VMEM((4, 4, SLAB, GIN), BF),
            pltpu.VMEM((2, 8, 144, 256), F32),
            pltpu.VMEM((8, 144, 256), F32),
            pltpu.VMEM((4, 2, 144, 256), F32),
            pltpu.VMEM((144, 256), F32),
            pltpu.VMEM((2, 8, 144, 256), BF),
            pltpu.VMEM((NSEQ, 2, TOK, 256), BF),
            pltpu.VMEM((TOK, 128), F32),
            dma((6,)),
            dma((STEPS, 2, 8)),
            dma((1,)),
            dma((19,)),
            dma((28,)),
            dma((28,)),
            dma((17,)),
        ],
        compiler_params=pltpu.CompilerParams(
            collective_id=0, has_side_effects=True, vmem_limit_bytes=60 * 1024 * 1024
        ),
        cost_estimate=pl.CostEstimate(flops=15_000_000_000, bytes_accessed=16_000_000, transcendentals=0),
    )(activations, grad_outputs, input_basis, output_basis, segment_ids)


def solution(mesh):
    placed = (P("row", "col"), P("col", "row"), P("col", "row"), P("row", "col"), P())
    return jax.shard_map(
        shards, mesh=mesh, in_specs=placed, out_specs=P("row", "col"), check_vma=False
    )
```

```python
import jax
import jax.numpy as jnp
from jax import lax
from jax.experimental import pallas as pl
from jax.experimental.pallas import tpu as pltpu
from jax.sharding import PartitionSpec as P

MESH = pl.DeviceIdType.MESH
NSEQ = 3
TOK = 1152
SLAB = 72
CIN = 1792
GIN = 512
STEPS = 7
WIDE = 256
QUARTER = 64
HALF = 32
PIECE = 16
LANES = ((0, 512), (512, 640))
LEAD = 1
GDONE = 24
LAGS = ((0, 2, 4, 6, 8, 10, 12), (0, 2, 4, 6, 8, 10, 12))
BF = jnp.bfloat16
F32 = jnp.float32


def kernel(
    act, grad, basis, obasis, ids, out,
    slabs, acts, bas, obas, part, half_out, half_in, full_out, full_in, z_out, z_in, rot, res,
    gslabs, gpart, gcore, gin, gpair, grot, gmask, labels,
    send, recv, asend, arecv, gsend, grecv, local,
):
    r, c = lax.axis_index("row"), lax.axis_index("col")
    core, x, zl = r % 2, (r // 2) % 4, r // 8
    y, zh = c % 4, c // 4

    def row_dev(x_, zl_, core_):
        return {"row": zl_ * 8 + x_ * 2 + core_, "col": c}

    def col_dev(y_, zh_):
        return {"row": r, "col": zh_ * 4 + y_}

    twin = row_dev(x, zl, 1 - core)
    x_up, x_dn = row_dev((x + 1) % 4, zl, core), row_dev((x + 3) % 4, zl, core)
    z_pair = row_dev(x, 1 - zl, core)
    y_up, y_dn = col_dev((y + 1) % 4, zh), col_dev((y + 3) % 4, zh)

    x_far = row_dev((x + 2) % 4, zl, core)

    barrier = pltpu.get_barrier_semaphore()
    for dev in [twin, x_up, x_dn, z_pair, x_far, y_up, y_dn] + [col_dev(y, (zh + o) % 4) for o in (1, 2, 3)]:
        pl.semaphore_signal(barrier, inc=1, device_id=dev, device_id_type=MESH)
    pl.semaphore_wait(barrier, 10)

    def remote(src, dst, s, d, dev):
        return pltpu.make_async_remote_copy(
            src_ref=src, dst_ref=dst, send_sem=s, recv_sem=d, device_id=dev, device_id_type=MESH
        )

    own_act = pltpu.make_async_copy(act, slabs.at[r], local.at[0])
    own_grad = pltpu.make_async_copy(grad, gslabs.at[zh, y], local.at[1])
    own_act.start()
    own_grad.start()
    own_ob = pltpu.make_async_copy(obasis, obas, local.at[2])
    own_ob.start()

    def basis_copy(j):
        return pltpu.make_async_copy(
            basis.at[:, pl.ds(pl.multiple_of(j * WIDE, WIDE), WIDE)], bas.at[j], local.at[3 + j]
        )

    def slab_at(x_, zl_, core_):
        return slabs.at[zl_ * 8 + x_ * 2 + core_]

    LO, HI = slice(0, CIN // 2), slice(CIN // 2, CIN)

    def ship(n, src, dst, dev):
        d = remote(src, dst, asend.at[0], arecv.at[n], dev)
        d.start()

    def landed(n, dst, dev):
        remote(dst, dst, asend.at[0], arecv.at[n], dev).wait_recv()

    xm, xp, xo, zo = (x + 3) % 4, (x + 1) % 4, (x + 2) % 4, 1 - zl
    mine = slabs.at[r]

    ship(0, act, mine, z_pair)
    ship(1, act.at[:, LO], mine.at[:, LO], x_up)
    ship(2, act.at[:, HI], mine.at[:, HI], x_dn)
    ship(17, act.at[:, HI], mine.at[:, HI], x_up)
    ship(18, act.at[:, LO], mine.at[:, LO], x_dn)
    ship(9, act, mine, twin)

    def gship(n, src, dst, dev):
        remote(src, dst, gsend.at[n], grecv.at[n], dev).start()

    def glanded(n, dst, dev):
        remote(dst, dst, gsend.at[n], grecv.at[n], dev).wait_recv()

    for j in range(STEPS):
        basis_copy(j).start()

    below, above, far = slab_at(xm, zl, core), slab_at(xp, zl, core), slab_at(xo, zl, core)
    landed(1, below.at[:, LO], x_dn)
    ship(5, below.at[:, LO], below.at[:, LO], x_up)
    landed(2, above.at[:, HI], x_up)
    ship(6, above.at[:, HI], above.at[:, HI], x_dn)
    landed(17, below.at[:, HI], x_dn)
    ship(11, below, below, twin)
    landed(18, above.at[:, LO], x_up)
    ship(12, above, above, twin)

    landed(0, slab_at(x, zo, core), z_pair)
    ship(3, slab_at(x, zo, core), slab_at(x, zo, core), x_up)
    ship(4, slab_at(x, zo, core), slab_at(x, zo, core), x_dn)
    ship(10, slab_at(x, zo, core), slab_at(x, zo, core), twin)

    for o in (1, 2, 3):
        h = (zh + o) % 4
        remote(grad, gslabs.at[zh, y], gsend.at[0], grecv.at[0], col_dev(y, h)).start()

    order = ((x, zl), (x, zo), (xm, zl), (xp, zl), (xo, zl), (xm, zo), (xp, zo), (xo, zo))

    def join(i):
        k = order[i][1] * 4 + order[i][0]
        a = slabs[2 * k].astype(F32)
        b = slabs[2 * k + 1].astype(F32)
        acts[pl.ds(i * 144, 144), :] = jnp.concatenate([a, b], axis=0).astype(BF)

    own_act.wait()
    for n, i in ((9, 0), (10, 1), (11, 2), (12, 3)):
        landed(n, slab_at(*order[i], 1 - core), twin)
        join(i)

    def act_far():
        landed(5, far.at[:, LO], x_dn)
        landed(6, far.at[:, HI], x_up)
        ship(7, far, far, z_pair)
        ship(15, far, far, twin)

    def act_cross():
        for n, x_, dev, out_n in ((3, xm, x_dn, 13), (4, xp, x_up, 14)):
            landed(n, slab_at(x_, zo, core), dev)
            ship(out_n, slab_at(x_, zo, core), slab_at(x_, zo, core), twin)

    def act_last():
        landed(7, slab_at(xo, zo, core), z_pair)
        ship(16, slab_at(xo, zo, core), slab_at(xo, zo, core), twin)
        for n, i in ((15, 4), (13, 5), (14, 6), (16, 7)):
            landed(n, slab_at(*order[i], 1 - core), twin)
            join(i)

    label = ids[...].reshape(1, TOK)
    weights = [
        1.0 / (jnp.sum((label == s).astype(F32), axis=1, keepdims=True) * NSEQ) for s in range(NSEQ)
    ]
    labels[...] = jnp.broadcast_to(label.astype(F32), (128, TOK)).T

    up, dn, op = (y + 1) % 4, (y + 3) % 4, (y + 2) % 4
    others = [(zh + o) % 4 for o in (1, 2, 3)]

    def msg(j, m, n_send, n_recv, src, dst, dev):
        return remote(src, dst, send.at[n_send], recv.at[j, m, n_recv], dev)

    def lanes(m):
        return pl.ds(*LANES[m])

    def stage_compute(j, m):
        ln = lanes(m)
        if m == 0:
            basis_copy(j).wait()
        prod = jnp.dot(acts[ln, :], bas[j], preferred_element_type=F32)
        part[j, :, :, ln] = prod.T.reshape(4, QUARTER, LANES[m][1])
        half_out[j, 0, :, ln] = part[j, op, :HALF, ln].astype(BF)
        half_out[j, 1, :, ln] = part[j, op, HALF:, ln].astype(BF)
        for n, dev in ((0, y_up), (1, y_dn)):
            msg(j, m, 0, n, half_out.at[j, n, :, ln], half_in.at[j, n, :, ln], dev).start()

    def stage_half(j, m):
        ln = lanes(m)
        msg(j, m, 0, 0, half_out.at[j, 0, :, ln], half_in.at[j, 0, :, ln], y_dn).wait_recv()
        full_out[j, 0, :HALF, ln] = (part[j, up, :HALF, ln] + half_in[j, 0, :, ln].astype(F32)).astype(BF)
        full_out[j, 0, HALF:, ln] = part[j, up, HALF:, ln].astype(BF)
        msg(j, m, 1, 2, full_out.at[j, 0, :, ln], full_in.at[j, 0, :, ln], y_up).start()
        msg(j, m, 0, 1, half_out.at[j, 1, :, ln], half_in.at[j, 1, :, ln], y_up).wait_recv()
        full_out[j, 1, HALF:, ln] = (part[j, dn, HALF:, ln] + half_in[j, 1, :, ln].astype(F32)).astype(BF)
        full_out[j, 1, :HALF, ln] = part[j, dn, :HALF, ln].astype(BF)
        msg(j, m, 1, 2, full_out.at[j, 1, :, ln], full_in.at[j, 1, :, ln], y_dn).start()

    def stage_full(j, m):
        ln = lanes(m)
        msg(j, m, 1, 2, full_out.at[j, :, :, ln], full_in.at[j, :, :, ln], y_dn).wait_recv()
        total = part[j, y, :, ln] + full_in[j, 0, :, ln].astype(F32) + full_in[j, 1, :, ln].astype(F32)
        part[j, y, :, ln] = total
        z_out[j, :, :, ln] = total.astype(BF).reshape(4, PIECE, LANES[m][1])
        for h in others:
            msg(j, m, 2, 3, z_out.at[j, h, :, ln], z_in.at[j, zh, :, ln], col_dev(y, h)).start()

    def stage_z(j, m):
        ln = lanes(m)
        total = part[j, y, pl.ds(pl.multiple_of(zh * PIECE, PIECE), PIECE), ln]
        msg(j, m, 2, 3, z_out.at[j, 0:3, :, ln], z_in.at[j, 0:3, :, ln], y_up).wait_recv()
        for h in others:
            total = total + z_in[j, h, :, ln].astype(F32)
        rot[j, y, zh, :, ln] = total.astype(BF)
        piece = rot.at[j, y, zh, :, ln]
        for h in others:
            msg(j, m, 3, 4, piece, piece, col_dev(y, h)).start()

    def stage_gather(j, m):
        ln = lanes(m)
        pieces = rot.at[j, y, 0:3, :, ln]
        msg(j, m, 3, 4, pieces, pieces, y_up).wait_recv()
        quarter = rot.at[j, y, :, :, ln]
        msg(j, m, 4, 5, quarter, quarter, y_up).start()
        msg(j, m, 4, 6, quarter, quarter, y_dn).start()

    def stage_relay(j, m):
        ln = lanes(m)
        below, above = rot.at[j, dn, :, :, ln], rot.at[j, up, :, :, ln]
        msg(j, m, 4, 5, below, below, y_dn).wait_recv()
        piece = rot.at[j, dn, 0:2, :, ln]
        msg(j, m, 5, 7, piece, piece, y_up).start()
        msg(j, m, 4, 6, above, above, y_up).wait_recv()
        piece = rot.at[j, up, 2:4, :, ln]
        msg(j, m, 5, 7, piece, piece, y_dn).start()

    def stage_last(j, m):
        ln = lanes(m)
        quarter = rot.at[j, op, :, :, ln]
        msg(j, m, 5, 7, quarter, quarter, y_dn).wait_recv()

    def out_copy(j):
        return pltpu.make_async_copy(
            res.at[j], out.at[pl.ds(pl.multiple_of(j * WIDE, WIDE), WIDE), :], local.at[10 + j]
        )

    def square(j):
        a = rot[j].reshape(WIDE, TOK)
        for h in range(2):
            total = None
            for s in range(NSEQ):
                p = jnp.dot(a, gmask[s, h], preferred_element_type=F32)
                term = p * p * weights[s]
                total = term if total is None else total + term
            res[j, :, pl.ds(h * 256, 256)] = total
        out_copy(j).start()

    def grad_y():
        own_grad.wait()
        remote(gslabs.at[0:3, 0], gslabs.at[0:3, 0], gsend.at[0], grecv.at[0], y_up).wait_recv()
        mine_y = gslabs.at[:, y]
        remote(mine_y, mine_y, gsend.at[0], grecv.at[1], y_up).start()
        remote(mine_y, mine_y, gsend.at[0], grecv.at[2], y_dn).start()

    def grad_relay():
        below_y, above_y = gslabs.at[:, dn], gslabs.at[:, up]
        remote(below_y, below_y, gsend.at[0], grecv.at[1], y_dn).wait_recv()
        piece = gslabs.at[0:2, dn]
        remote(piece, piece, gsend.at[0], grecv.at[3], y_up).start()
        remote(above_y, above_y, gsend.at[0], grecv.at[2], y_up).wait_recv()
        piece = gslabs.at[2:4, up]
        remote(piece, piece, gsend.at[0], grecv.at[3], y_dn).start()

    def grad_rotate():
        remote(gslabs.at[:, op], gslabs.at[:, op], gsend.at[0], grecv.at[3], y_up).wait_recv()
        own_ob.wait()

        def rotate(k, carry):
            a = gslabs[k // 2, 2 * (k % 2)].astype(F32)
            b = gslabs[k // 2, 2 * (k % 2) + 1].astype(F32)
            both = jnp.concatenate([a, b], axis=0).astype(BF)
            prod = jnp.dot(both, obas[...], preferred_element_type=F32)
            gpart[0, k] = prod[:, :256]
            gpart[1, k] = prod[:, 256:]
            return carry

        lax.fori_loop(0, 8, rotate, 0)
        gship(16, gpart.at[1 - core], gcore, twin)

    def x_dev(x_):
        return row_dev(x_, zl, core)

    def grad_core():
        glanded(16, gcore, twin)

        def add(k, carry):
            gpart[core, k] = gpart[core, k] + gcore[k]
            return carry

        lax.fori_loop(0, 8, add, 0)
        for o in (1, 2, 3):
            k = (x + o) % 4
            pair = gpart.at[core, pl.ds(2 * k, 2)]
            remote(pair, gin.at[x], gsend.at[17], grecv.at[17], x_dev(k)).start()

    def grad_x():
        glanded(17, gin.at[0:3], x_up)
        for o in (1, 2, 3):
            k = (x + o) % 4
            for i in range(2):
                gpart[core, 2 * x + i] = gpart[core, 2 * x + i] + gin[k, i]
        gship(21, gpart.at[core, 2 * x + zo], gpair, z_pair)

    def grad_sum():
        glanded(21, gpair, z_pair)
        grot[core, 2 * x + zl] = (gpart[core, 2 * x + zl] + gpair[...]).astype(BF)
        piece = grot.at[core, 2 * x + zl]
        gship(22, piece, piece, z_pair)

    def grad_z():
        glanded(22, grot.at[core, 2 * x + zo], z_pair)
        pair = grot.at[core, pl.ds(2 * x, 2)]
        for o in (1, 2, 3):
            k = (x + o) % 4
            remote(pair, pair, gsend.at[23], grecv.at[23], x_dev(k)).start()

    def grad_gather():
        glanded(23, grot.at[core, 0:6], x_up)
        gship(27, grot.at[core], grot.at[core], twin)

    def grad_done():
        glanded(27, grot.at[1 - core], twin)
        for i in range(8):
            k = order[i][1] * 4 + order[i][0]
            rows = labels[pl.ds(pl.multiple_of(k * 144, 16), 144), :]
            for s in range(NSEQ):
                member = (rows == s).astype(F32).astype(BF)
                member = jnp.concatenate([member, member], axis=1)
                for h in range(2):
                    gmask[s, h, pl.ds(i * 144, 144), :] = grot[h, k] * member
        lax.fori_loop(0, 2, lambda j, carry: (square(j), carry)[1], 0)

    def late_squares():
        lax.fori_loop(2, (GDONE - LAGS[1][-1]) // 2 - LEAD, lambda j, carry: (square(j), carry)[1], 0)

    stages = [stage_compute, stage_half, stage_full, stage_z, stage_gather, stage_relay, stage_last]
    deep = LAGS[1][-1]
    extras = (
        (0, act_far), (2, grad_y), (2, act_cross), (2, act_last), (5, grad_relay), (8, grad_rotate), (9, grad_core), (14, grad_x), (16, grad_sum), (18, grad_z), (21, grad_gather), (GDONE, grad_done), (GDONE + 2, late_squares),
    )

    def turn(pair, carry):
        for parity in range(2):
            now = 2 * pair + parity
            for k, stage in enumerate(stages):
                for m in range(2):
                    lag = LAGS[m][k]
                    if (parity + lag + m) % 2:
                        continue
                    j = (now - lag - m) // 2 - m * LEAD

                    @pl.when((j >= 0) & (j < STEPS))
                    def _():
                        stage(j, m)
                        if k == len(stages) - 1 and m == 1:
                            pl.when(now >= GDONE)(lambda: square(j))

            for at, extra in extras:
                if at % 2 == parity:
                    pl.when(now == at)(extra)

        return carry

    lax.fori_loop(0, (2 * (STEPS - 1 + LEAD) + 1 + deep) // 2 + 1, turn, 0)

    for j in range(STEPS):
        out_copy(j).wait()

    def sent(sem, ref):
        remote(ref, ref, sem, sem, twin).wait_send()

    sent(send.at[0], half_out)
    sent(send.at[1], full_out)
    sent(send.at[2], z_out.at[:, 0:3])
    sent(send.at[3], z_out.at[:, 0:3])
    sent(send.at[4], rot.at[:, 0:2])
    sent(send.at[5], rot.at[:, 0])
    sent(asend.at[0], slabs.at[0:15])
    sent(gsend.at[0], gslabs.at[0:3])
    sent(gsend.at[0], gslabs.at[0, 0:3])
    sent(gsend.at[16], gcore)
    sent(gsend.at[17], gin.at[0:3])
    sent(gsend.at[21], gpair)
    sent(gsend.at[22], grot.at[core, 0])
    sent(gsend.at[23], grot.at[core, 0:6])
    sent(gsend.at[27], grot.at[core])


def shards(activations, grad_outputs, input_basis, output_basis, segment_ids):
    hbm = pl.BlockSpec(memory_space=pl.ANY)
    dma = pltpu.SemaphoreType.DMA
    return pl.pallas_call(
        kernel,
        out_shape=jax.ShapeDtypeStruct((CIN, GIN), F32),
        in_specs=[hbm, hbm, hbm, hbm, pl.BlockSpec(memory_space=pltpu.VMEM)],
        out_specs=hbm,
        scratch_shapes=[
            pltpu.VMEM((16, SLAB, CIN), BF),
            pltpu.VMEM((TOK, CIN), BF),
            pltpu.VMEM((STEPS, CIN, WIDE), BF),
            pltpu.VMEM((GIN, GIN), BF),
            pltpu.VMEM((STEPS, 4, QUARTER, TOK), F32),
            pltpu.VMEM((STEPS, 2, HALF, TOK), BF),
            pltpu.VMEM((STEPS, 2, HALF, TOK), BF),
            pltpu.VMEM((STEPS, 2, QUARTER, TOK), BF),
            pltpu.VMEM((STEPS, 2, QUARTER, TOK), BF),
            pltpu.VMEM((STEPS, 4, PIECE, TOK), BF),
            pltpu.VMEM((STEPS, 4, PIECE, TOK), BF),
            pltpu.VMEM((STEPS, 4, 4, PIECE, TOK), BF),
            pltpu.VMEM((STEPS, WIDE, GIN), F32),
            pltpu.VMEM((4, 4, SLAB, GIN), BF),
            pltpu.VMEM((2, 8, 144, 256), F32),
            pltpu.VMEM((8, 144, 256), F32),
            pltpu.VMEM((4, 2, 144, 256), F32),
            pltpu.VMEM((144, 256), F32),
            pltpu.VMEM((2, 8, 144, 256), BF),
            pltpu.VMEM((NSEQ, 2, TOK, 256), BF),
            pltpu.VMEM((TOK, 128), F32),
            dma((6,)),
            dma((STEPS, 2, 8)),
            dma((1,)),
            dma((19,)),
            dma((28,)),
            dma((28,)),
            dma((17,)),
        ],
        compiler_params=pltpu.CompilerParams(
            collective_id=0, has_side_effects=True, vmem_limit_bytes=60 * 1024 * 1024
        ),
        cost_estimate=pl.CostEstimate(flops=15_000_000_000, bytes_accessed=16_000_000, transcendentals=0),
    )(activations, grad_outputs, input_basis, output_basis, segment_ids)


def solution(mesh):
    placed = (P("row", "col"), P("col", "row"), P("col", "row"), P("row", "col"), P())
    return jax.shard_map(
        shards, mesh=mesh, in_specs=placed, out_specs=P("row", "col"), check_vma=False
    )
```
